512 devices in a mesh: space: 16 (over z_lo, x), wide: 32 (over y, z_hi, core).
Axes of the slice: x: 4, y: 8, z: 8 (z_hi: 2, z_lo: 4; z = z_hi * 4 + z_lo), core: 2. Of those that a mesh axis runs over, the one named last changes fastest.
Arguments:
- latent: bfloat16 [32, 16, 4, 128, 128], P('wide', 'space'), may hold values from -6 to 6
- coords: bfloat16 [32, 16, 4, 2, 128], P('wide', 'space'), may hold values from 0 to 1
- cell_counts: int32 [32, 16, 4], P('wide', 'space'), may hold values from 32 to 128, as said below
- pair_target: int32 [32, 16, 12], P('wide', 'space'), may hold values from 0 to 3, as said below
- pair_source: int32 [32, 16, 12], P('wide', 'space'), may hold values from 0 to 5, as said below
- pair_count: int32 [32, 16], P('wide', 'space'), may hold values from 3 to 12, as said below
- edge_target_w: bfloat16 [128, 128], replicated, may hold values from -0.5 to 0.5
- edge_source_w: bfloat16 [128, 128], replicated, may hold values from -0.5 to 0.5
- edge_offset: float32 [2, 128], replicated, may hold values from -4 to 4
- edge_bias: float32 [128], replicated, may hold values from -4 to 4
- edge_out: bfloat16 [128, 128], replicated, may hold values from -0.0234375 to 0.0234375
- node_in: bfloat16 [256, 128], replicated, may hold values from -0.375 to 0.375
- node_in_bias: float32 [128], replicated, may hold values from -4 to 4
- node_out: bfloat16 [128, 128], replicated, may hold values from -0.5 to 0.5
- node_out_bias: float32 [128], replicated, may hold values from -4 to 4
- norm_gain: float32 [128], replicated, may hold values from 0.25 to 1.75
- cotangent: bfloat16 [32, 16, 4, 128, 128], P('wide', 'space'), may hold values from -6 to 6
Outputs:
- new_latent: bfloat16 [32, 16, 4, 128, 128], P('wide', 'space')
- latent_grad: float32 [32, 16, 4, 128, 128], P('wide', 'space')
- grad_target_w: float32 [128, 128], replicated
- grad_source_w: float32 [128, 128], replicated
- grad_offset: float32 [2, 128], replicated
- grad_bias: float32 [128], replicated
- grad_edge_out: float32 [128, 128], replicated
- grad_node_in: float32 [256, 128], replicated
- grad_in_bias: float32 [128], replicated
- grad_node_out: float32 [128, 128], replicated
- grad_out_bias: float32 [128], replicated
- grad_gain: float32 [128], replicated
The draws below stay inside these ranges and needn't reach their ends.
Inputs may be any that keep to these rules, and one draw needn't show every extreme that they name: Live particles of a cell are its first cell_counts slots; some cell of the domain is full. The 12 slots of one device name distinct pairs; pair_source - pair_target is 0, 1 or 2, so a source is the target cell, the one before or the one after along the strip. Slots from pair_count on hold valid pairs that are not used. `pair_source`: window index: 0 is the last cell of the previous space index, 1 to 4 the device's own cells, 5 the first cell of the next space index. `pair_count`: each device lists 3, 6 or 12 pairs; some device lists 12.
All inputs are finite; a program needn't handle non-finite values.
Results may differ from the reference program's by a relative error of at most 0.0083.
Values may be sent and summed in bfloat16 or wider, within the bound.
No kernel may reach another device: no remote copies, remote signals or barrier semaphores. Data moves between devices by JAX's collectives and lax.ppermute only.
A program may use at most 64 MiB of HBM per device.

```python
import math
import jax
import jax.numpy as jnp
from jax import lax

LAT = 128
HID = 128
NH = 128
PART = 128
CD = 4
PMAX = 12
N_SPACE = 16
N_WIDE = 32


def pair_table(key):
    devices_all = N_WIDE * N_SPACE
    score_key, level_key, pick_key = jax.random.split(key, 3)
    scores = jax.random.randint(score_key, (devices_all, PMAX), 0, 1 << 20) * PMAX + jnp.arange(PMAX, dtype=jnp.int32)[None, :]
    ranking = jnp.argsort(scores, axis=1, stable=True).astype(jnp.int32)
    targets = ranking // 3
    sources = targets + ranking % 3
    levels = jax.random.randint(level_key, (devices_all,), 0, 3)
    counts = PMAX // 4 * jnp.left_shift(jnp.ones_like(levels), levels)
    chosen = jax.random.randint(pick_key, (), 0, devices_all)
    counts = jnp.where(jnp.arange(devices_all) == chosen, PMAX, counts).astype(jnp.int32)
    return (targets.reshape(N_WIDE, N_SPACE, PMAX), sources.reshape(N_WIDE, N_SPACE, PMAX), counts.reshape(N_WIDE, N_SPACE))


def draw_pair_target(key, part):
    table = pair_table(key)
    return table[0]


def draw_pair_source(key, part):
    table = pair_table(key)
    return table[1]


def draw_pair_count(key, part):
    table = pair_table(key)
    return table[2]


def draw_cell_counts(key, part):
    key = jax.random.fold_in(key, 4)
    count_key, pick_key = jax.random.split(key)
    total_cells = N_WIDE * N_SPACE * CD
    values = jax.random.randint(count_key, (total_cells,), PART // 4, PART + 1)
    chosen = jax.random.randint(pick_key, (), 0, total_cells)
    values = jnp.where(jnp.arange(total_cells) == chosen, PART, values).astype(jnp.int32)
    return values.reshape(N_WIDE, N_SPACE, CD)


def shard_levels(rng, dims, cuts, least, top_value):
    def one(dim, shards_of):
        steps = jax.random.uniform(jax.random.fold_in(jax.random.fold_in(rng, 6), dim), (shards_of,), jnp.float32, least / len(cuts), top_value / len(cuts))
        return jnp.repeat(jnp.exp(steps), dims[dim] // shards_of).reshape((-1,) + (1,) * (len(dims) - dim - 1))

    loudness = one(*cuts[0])
    for cut in cuts[1:]:
        loudness = loudness * one(*cut)
    return loudness


def noise(own_key, dims, deviation, most, cuts=(), kind=jnp.bfloat16):
    loudness = shard_levels(own_key, dims, cuts, -0.22, 0.18) if cuts else 1.0
    values = jax.random.normal(own_key, dims, jnp.float32) * deviation * loudness
    return jnp.minimum(jnp.maximum(values, -most), most).astype(kind)


def setup_inputs(seed: int = 0) -> dict:
    key_of = jax.random.split(jax.random.key(seed), 18)
    return {
        "latent": noise(key_of[0], (N_WIDE, N_SPACE, CD, PART, LAT), 1.0, 6.0, ((0, 32), (1, 16))),
        "coords": jnp.clip(1.0 * jax.random.uniform(key_of[1], (N_WIDE, N_SPACE, CD, 2, PART), jnp.float32) ** shard_levels(key_of[1], (N_WIDE, N_SPACE, CD, 2, PART), ((0, 32), (1, 16)), -0.2, 0.2), 0.0, 1.0).astype(jnp.bfloat16),
        "cell_counts": draw_cell_counts(jax.random.fold_in(key_of[17], 71), 0),
        "pair_target": draw_pair_target(jax.random.fold_in(key_of[17], 71), 0),
        "pair_source": draw_pair_source(jax.random.fold_in(key_of[17], 71), 0),
        "pair_count": draw_pair_count(jax.random.fold_in(key_of[17], 71), 0),
        "edge_target_w": noise(key_of[6], (LAT, HID), LAT ** -0.5, 0.5),
        "edge_source_w": noise(key_of[7], (LAT, HID), LAT ** -0.5, 0.5),
        "edge_offset": noise(key_of[8], (2, HID), 2 ** -0.5, 4.0, (), jnp.float32),
        "edge_bias": noise(key_of[9], (HID,), 1.0, 4.0, (), jnp.float32),
        "edge_out": noise(key_of[10], (HID, LAT), (HID * PART * 4) ** -0.5, 0.0234375),
        "node_in": noise(key_of[11], (2 * LAT, NH), (2 * LAT) ** -0.5, 0.375),
        "node_in_bias": noise(key_of[12], (NH,), 1.0, 4.0, (), jnp.float32),
        "node_out": noise(key_of[13], (NH, LAT), NH ** -0.5, 0.5),
        "node_out_bias": noise(key_of[14], (LAT,), 1.0, 4.0, (), jnp.float32),
        "norm_gain": jnp.clip(1.0 + 0.15 * jax.random.normal(key_of[15], (LAT,), jnp.float32), 0.25, 1.75),
        "cotangent": noise(key_of[16], (N_WIDE, N_SPACE, CD, PART, LAT), 1.0, 6.0, ((0, 32), (1, 16))),
    }


def silu_slope(values):
    sigma = jax.nn.sigmoid(values)
    return sigma * (1.0 + values * (1.0 - sigma))

def tile_geometry(own_coords, window_coords, own_live, window_live, target, source):
    target_xy = lax.dynamic_index_in_dim(own_coords, target, 0, False).astype(jnp.float32)
    source_xy = lax.dynamic_index_in_dim(window_coords, source, 0, False).astype(jnp.float32)
    target_live = lax.dynamic_index_in_dim(own_live, target, 0, False).astype(jnp.float32)
    source_live = lax.dynamic_index_in_dim(window_live, source, 0, False).astype(jnp.float32)
    offset_cells = (target - source + 1).astype(jnp.float32)
    delta_x = offset_cells + target_xy[0][:, None] - source_xy[0][None, :]
    delta_y = target_xy[1][:, None] - source_xy[1][None, :]
    falloff = jnp.maximum(1.0 - delta_x * delta_x - delta_y * delta_y, 0.0)
    weight = falloff * falloff * target_live[:, None] * source_live[None, :]
    return (delta_x, delta_y, weight)

def tile_preact(own_proj, window_proj, edge_offset, target, source, delta_x, delta_y):
    target_rows = lax.dynamic_index_in_dim(own_proj, target, 0, False).astype(jnp.float32)
    source_rows = lax.dynamic_index_in_dim(window_proj, source, 0, False).astype(jnp.float32)
    return target_rows[:, None, :] + source_rows[None, :, :] + delta_x[:, :, None] * edge_offset[0] + delta_y[:, :, None] * edge_offset[1]

def edge_forward(own_proj, window_proj, own_coords, window_coords, own_live, window_live, targets, sources, live_pairs, slot_stop, edge_offset):

    def visit(slot_index, running):
        target = targets[slot_index].astype(jnp.int32)
        source = sources[slot_index].astype(jnp.int32)
        delta_x, delta_y, weight = tile_geometry(own_coords, window_coords, own_live, window_live, target, source)
        preact = tile_preact(own_proj, window_proj, edge_offset, target, source, delta_x, delta_y)
        active = (slot_index < live_pairs).astype(jnp.float32)
        contrib = lax.optimization_barrier(jnp.sum(weight[:, :, None] * jax.nn.silu(preact), axis=1)) * active
        current = lax.dynamic_index_in_dim(running, target, 0, False)
        return lax.dynamic_update_index_in_dim(running, current + contrib, target, 0)
    return lax.fori_loop(0, slot_stop, visit, jnp.zeros(own_proj.shape, jnp.float32))

def edge_backward(own_proj, window_proj, own_coords, window_coords, own_live, window_live, targets, sources, live_pairs, slot_stop, edge_offset, upstream):

    def visit(slot_index, carry):
        grad_own, grad_window, grad_offset = carry
        target = targets[slot_index].astype(jnp.int32)
        source = sources[slot_index].astype(jnp.int32)
        delta_x, delta_y, weight = tile_geometry(own_coords, window_coords, own_live, window_live, target, source)
        preact = tile_preact(own_proj, window_proj, edge_offset, target, source, delta_x, delta_y)
        active = (slot_index < live_pairs).astype(jnp.float32)
        upstream_rows = lax.dynamic_index_in_dim(upstream, target, 0, False)
        gated = silu_slope(preact) * weight[:, :, None] * upstream_rows[:, None, :] * active
        own_rows = lax.dynamic_index_in_dim(grad_own, target, 0, False) + lax.optimization_barrier(jnp.sum(gated, axis=1))
        grad_own = lax.dynamic_update_index_in_dim(grad_own, own_rows, target, 0)
        window_rows = lax.dynamic_index_in_dim(grad_window, source, 0, False) + lax.optimization_barrier(jnp.sum(gated, axis=0))
        grad_window = lax.dynamic_update_index_in_dim(grad_window, window_rows, source, 0)
        along = lax.optimization_barrier(jnp.sum(gated * delta_x[:, :, None], axis=(0, 1)))
        across = lax.optimization_barrier(jnp.sum(gated * delta_y[:, :, None], axis=(0, 1)))
        grad_offset = grad_offset + jnp.stack([along, across])
        return (grad_own, grad_window, grad_offset)
    start = (jnp.zeros(own_proj.shape, jnp.float32), jnp.zeros(window_proj.shape, jnp.float32), jnp.zeros(edge_offset.shape, jnp.float32))
    return lax.fori_loop(0, slot_stop, visit, start)

def node_forward(flat_rows, aggregate, edge_out, node_in, node_in_bias, node_out, node_out_bias, norm_gain):
    latent_width = flat_rows.shape[1]
    agg_b = aggregate.astype(jnp.bfloat16)
    message_b = jnp.dot(agg_b, edge_out, preferred_element_type=jnp.float32).astype(jnp.bfloat16)
    hidden_pre = jnp.dot(flat_rows, node_in[:latent_width], preferred_element_type=jnp.float32) + jnp.dot(message_b, node_in[latent_width:], preferred_element_type=jnp.float32) + node_in_bias
    hidden = jax.nn.silu(hidden_pre)
    hidden_b = hidden.astype(jnp.bfloat16)
    pre_norm = jnp.dot(hidden_b, node_out, preferred_element_type=jnp.float32) + node_out_bias
    row_mean = lax.optimization_barrier(jnp.mean(pre_norm, axis=-1, keepdims=True))
    centred = pre_norm - row_mean
    row_var = lax.optimization_barrier(jnp.mean(centred * centred, axis=-1, keepdims=True))
    inverse = lax.rsqrt(row_var + 1e-05)
    normed = centred * inverse
    new_rows = (flat_rows.astype(jnp.float32) + normed * norm_gain).astype(jnp.bfloat16)
    return (new_rows, (agg_b, message_b, hidden_pre, hidden_b, normed, inverse))

def node_backward(flat_rows, cotangent_rows, saved, edge_out, node_in, node_out, norm_gain):
    agg_b, message_b, hidden_pre, hidden_b, normed, inverse = saved
    latent_width = flat_rows.shape[1]
    cotangent_f = cotangent_rows.astype(jnp.float32)
    grad_gain = lax.optimization_barrier(jnp.sum(cotangent_f * normed, axis=0))
    grad_normed = cotangent_f * norm_gain
    grad_pre = inverse * (grad_normed - lax.optimization_barrier(jnp.mean(grad_normed, axis=-1, keepdims=True)) - normed * lax.optimization_barrier(jnp.mean(grad_normed * normed, axis=-1, keepdims=True)))
    grad_pre_b = grad_pre.astype(jnp.bfloat16)
    grad_out_bias = lax.optimization_barrier(jnp.sum(grad_pre, axis=0))
    grad_node_out = jnp.dot(hidden_b.T, grad_pre_b, preferred_element_type=jnp.float32)
    grad_hidden = jnp.dot(grad_pre_b, node_out.T, preferred_element_type=jnp.float32) * silu_slope(hidden_pre)
    grad_hidden_b = grad_hidden.astype(jnp.bfloat16)
    grad_in_bias = lax.optimization_barrier(jnp.sum(grad_hidden, axis=0))
    grad_node_in = jnp.concatenate([jnp.dot(flat_rows.T, grad_hidden_b, preferred_element_type=jnp.float32), jnp.dot(message_b.T, grad_hidden_b, preferred_element_type=jnp.float32)], axis=0)
    grad_message_b = jnp.dot(grad_hidden_b, node_in[latent_width:].T, preferred_element_type=jnp.float32).astype(jnp.bfloat16)
    grad_edge_out = jnp.dot(agg_b.T, grad_message_b, preferred_element_type=jnp.float32)
    grad_aggregate = jnp.dot(grad_message_b, edge_out.T, preferred_element_type=jnp.float32)
    grad_rows = cotangent_f + jnp.dot(grad_hidden_b, node_in[:latent_width].T, preferred_element_type=jnp.float32)
    return (grad_aggregate, grad_rows, (grad_edge_out, grad_node_in, grad_in_bias, grad_node_out, grad_out_bias, grad_gain))

def strip_window(values):
    earlier = jnp.concatenate([jnp.zeros_like(values[:, :1, -1:]), values[:, :-1, -1:]], axis=1)
    following = jnp.concatenate([values[:, 1:, :1], jnp.zeros_like(values[:, :1, :1])], axis=1)
    return jnp.concatenate([earlier, values, following], axis=2)

def reference(latent, coords, cell_counts, pair_target, pair_source, pair_count, edge_target_w, edge_source_w, edge_offset, edge_bias, edge_out, node_in, node_in_bias, node_out, node_out_bias, norm_gain, cotangent):
    strips, spans, cells, particles, latent_width = latent.shape
    hidden_width = edge_target_w.shape[1]
    devices_all = strips * spans
    slot_stop = pair_target.shape[-1]
    flat_rows = latent.reshape(-1, latent_width)
    own_proj = (jnp.dot(flat_rows, edge_target_w, preferred_element_type=jnp.float32) + edge_bias).astype(jnp.bfloat16).reshape(strips, spans, cells, particles, hidden_width)
    source_proj = jnp.dot(flat_rows, edge_source_w, preferred_element_type=jnp.float32).astype(jnp.bfloat16).reshape(strips, spans, cells, particles, hidden_width)
    live_mask = (jnp.arange(particles, dtype=jnp.int32)[None, None, None, :] < cell_counts[..., None]).astype(jnp.bfloat16)

    def per_device(values):
        return values.reshape((devices_all,) + values.shape[2:])
    pieces = (per_device(own_proj), per_device(strip_window(source_proj)), per_device(coords), per_device(strip_window(coords)), per_device(live_mask), per_device(strip_window(live_mask)), per_device(pair_target), per_device(pair_source), per_device(pair_count))

    def forward_device(items):
        return edge_forward(items[0], items[1], items[2], items[3], items[4], items[5], items[6], items[7], items[8], slot_stop, edge_offset)
    aggregate = lax.map(forward_device, pieces)
    new_rows, saved = node_forward(flat_rows, aggregate.reshape(-1, hidden_width), edge_out, node_in, node_in_bias, node_out, node_out_bias, norm_gain)
    grad_aggregate, grad_rows, node_grads = node_backward(flat_rows, cotangent.reshape(-1, latent_width), saved, edge_out, node_in, node_out, norm_gain)
    upstream = grad_aggregate.reshape(devices_all, cells, particles, hidden_width)

    def backward_device(items):
        return edge_backward(items[0], items[1], items[2], items[3], items[4], items[5], items[6], items[7], items[8], slot_stop, edge_offset, items[9])
    grad_target, grad_window, grad_offsets = lax.map(backward_device, pieces + (upstream,))
    grad_offset = lax.optimization_barrier(jnp.sum(grad_offsets, axis=0))
    grad_window = grad_window.reshape(strips, spans, cells + 2, particles, hidden_width)
    from_next = jnp.concatenate([grad_window[:, 1:, 0], jnp.zeros_like(grad_window[:, :1, 0])], axis=1)
    from_prev = jnp.concatenate([jnp.zeros_like(grad_window[:, :1, cells + 1]), grad_window[:, :-1, cells + 1]], axis=1)
    grad_source = grad_window[:, :, 1:cells + 1].at[:, :, cells - 1].add(from_next).at[:, :, 0].add(from_prev)
    target_flat = grad_target.reshape(-1, hidden_width)
    target_b = target_flat.astype(jnp.bfloat16)
    source_b = grad_source.reshape(-1, hidden_width).astype(jnp.bfloat16)
    grad_target_w = jnp.dot(flat_rows.T, target_b, preferred_element_type=jnp.float32)
    grad_source_w = jnp.dot(flat_rows.T, source_b, preferred_element_type=jnp.float32)
    grad_bias = lax.optimization_barrier(jnp.sum(target_flat, axis=0))
    grad_rows = grad_rows + jnp.dot(target_b, edge_target_w.T, preferred_element_type=jnp.float32) + jnp.dot(source_b, edge_source_w.T, preferred_element_type=jnp.float32)
    grad_edge_out, grad_node_in, grad_in_bias, grad_node_out, grad_out_bias, grad_gain = node_grads
    grad_scale = 1.0 / math.sqrt(devices_all * cells * particles)
    return (new_rows.reshape(latent.shape), grad_rows.reshape(latent.shape), grad_target_w * grad_scale, grad_source_w * grad_scale, grad_offset * grad_scale, grad_bias * grad_scale, grad_edge_out * grad_scale, grad_node_in * grad_scale, grad_in_bias * grad_scale, grad_node_out * grad_scale, grad_out_bias * grad_scale, grad_gain * grad_scale)
```

```python
import functools
import math

import jax
import jax.numpy as jnp
from jax import lax
from jax.experimental import pallas as pl
from jax.experimental.pallas import tpu as pltpu
from jax.sharding import PartitionSpec as P

BF = jnp.bfloat16
F32 = jnp.float32
META = 16
GRAIN = 16
PACK_ROWS = 800


def dot(a, b):
    return jnp.dot(a, b, preferred_element_type=F32)


def dot_t(a, b):
    return lax.dot_general(a, b, (((1,), (1,)), ((), ())), preferred_element_type=F32)


def t_dot(a, b):
    return lax.dot_general(a, b, (((0,), (0,)), ((), ())), preferred_element_type=F32)


def sigmoid(v):
    return 0.5 * (1.0 + jnp.tanh(0.5 * v))


def blocks(count):
    return lax.div(count + (GRAIN - 1), GRAIN)


def column_sum(values):
    return jnp.sum(values, axis=0, keepdims=True)


def step_kernel(
    counts_ref,
    targets_ref,
    sources_ref,
    listed_ref,
    latent_ref,
    meta_ref,
    before_ref,
    after_ref,
    target_w_ref,
    source_w_ref,
    offset_ref,
    bias_ref,
    edge_out_ref,
    node_in_ref,
    node_in_bias_ref,
    node_out_ref,
    node_out_bias_ref,
    gain_ref,
    cotangent_ref,
    new_latent_ref,
    latent_grad_ref,
    rim_grad_ref,
    pack_ref,
    live_ref,
    place_ref,
    x_ref,
    y_ref,
    a_base_ref,
    b_base_ref,
    weight_ref,
    weight_t_ref,
    aggregate_ref,
    slope_ref,
    slope_shift_ref,
    upstream_ref,
    source_grad_ref,
    a_ref,
    a_half_ref,
    b_ref,
    b_half_ref,
    pair_sum_ref,
    shift_ref,
):
    cells, particles, width = latent_ref.shape[2:]
    rows = cells * particles
    offset_x = offset_ref[0:1, :]
    offset_y = offset_ref[1:2, :]

    for cell in range(cells):
        live_ref[cell + 1] = counts_ref[0, 0, cell]
        place_ref[cell + 1] = meta_ref[cell].astype(F32)
    place_ref[0] = before_ref[particles:, :].astype(F32)
    place_ref[cells + 1] = after_ref[particles:, :].astype(F32)
    live_ref[0] = jnp.sum(place_ref[0, 2:3, :]).astype(jnp.int32)
    live_ref[cells + 1] = jnp.sum(place_ref[cells + 1, 2:3, :]).astype(jnp.int32)

    pick = lax.broadcasted_iota(jnp.int32, (META, width), 0)
    pick_x = jnp.where(pick == 0, 1.0, 0.0).astype(BF)
    pick_y = jnp.where(pick == 1, 1.0, 0.0).astype(BF)
    for slot in range(cells + 2):
        if slot == 0:
            rows_in = before_ref[:particles, :]
        elif slot == cells + 1:
            rows_in = after_ref[:particles, :]
        else:
            rows_in = latent_ref[0, 0, slot - 1]
        place = place_ref[slot].astype(BF)
        x = t_dot(place, pick_x)
        y = t_dot(place, pick_y)
        x_ref[slot] = x
        y_ref[slot] = y
        moved = x * offset_x + (y - 0.5) * offset_y
        proj_source = dot(rows_in, source_w_ref[...]).astype(BF).astype(F32)
        b_base_ref[slot] = 0.5 * (proj_source - moved)
        if 0 < slot < cells + 1:
            proj_target = (dot(rows_in, target_w_ref[...]) + bias_ref[...]).astype(BF)
            a_base_ref[slot - 1] = 0.5 * (proj_target.astype(F32) + moved)

    aggregate_ref[...] = jnp.zeros_like(aggregate_ref)
    slope_ref[...] = jnp.zeros_like(slope_ref)
    slope_shift_ref[...] = jnp.zeros_like(slope_shift_ref)
    source_grad_ref[...] = jnp.zeros_like(source_grad_ref)
    shift_ref[...] = jnp.zeros_like(shift_ref)

    row_of = lax.broadcasted_iota(jnp.int32, (GRAIN, width), 0)
    sub = lax.broadcasted_iota(jnp.int32, (particles, particles), 0)
    lane = lax.broadcasted_iota(jnp.int32, (particles, particles), 1)
    listed = listed_ref[0, 0]

    def pair_of(slot):
        target = targets_ref[0, 0, slot]
        source = sources_ref[0, 0, slot]
        off = (target - source + 1).astype(F32)
        alpha = jnp.where(off < -0.5, -1.0, jnp.where(off > 0.5, 0.0, -0.5))
        return target, source, off, alpha, off - alpha

    def set_pair(target, source, alpha, beta):
        a = a_base_ref[target] + (0.5 * alpha) * offset_x
        b = b_base_ref[source] + (0.5 * beta) * offset_x
        a_ref[...] = a
        b_ref[...] = b
        a_half_ref[...] = a.astype(BF)
        b_half_ref[...] = b.astype(BF)

    def over_sizes(count, visit):
        for size in range(2 * GRAIN, particles + 1, GRAIN):
            pl.when(blocks(count) == size // GRAIN)(functools.partial(visit, size))

    def forward_pair(slot, _):
        target, source, off, alpha, beta = pair_of(slot)
        live_target = live_ref[target + 1]
        live_source = live_ref[source]

        @pl.when(live_source > 0)
        def _():
            set_pair(target, source, alpha, beta)
            dx = (off + x_ref[target + 1]) - place_ref[source, 0:1, :]
            dy = y_ref[target + 1] - place_ref[source, 1:2, :]
            near = jnp.maximum(1.0 - dx * dx - dy * dy, 0.0)
            keep = (sub < live_target) & (lane < live_source)
            weight = jnp.where(keep, near * near, 0.0).astype(BF)
            weight_ref[slot] = weight
            dx = (off + place_ref[target + 1, 0:1, :]) - x_ref[source]
            dy = place_ref[target + 1, 1:2, :] - y_ref[source]
            near = jnp.maximum(1.0 - dx * dx - dy * dy, 0.0)
            keep = (lane < live_target) & (sub < live_source)
            weight_t_ref[slot] = jnp.where(keep, near * near, 0.0).astype(BF)
            ones = jnp.ones((particles, width), BF)
            linear = dot(weight, jnp.concatenate([b_half_ref[...], ones], axis=1))
            weight_sum = linear[:, width:]
            aggregate_ref[target] += a_ref[...] * weight_sum + linear[:, :width]
            pair_sum_ref[...] = weight_sum

            def visit(size):
                def block(index, _):
                    first = pl.multiple_of(index * GRAIN, GRAIN)
                    here = pl.ds(first, GRAIN)
                    weights = weight_ref[slot, here, :]
                    b = b_half_ref[0:size, :]
                    total = jnp.zeros((GRAIN, 2 * width), F32)
                    for r in range(GRAIN):
                        a = a_ref[pl.ds(first + r, 1), :].astype(BF)
                        u = jnp.broadcast_to(a, (size, width)) + b
                        t = jnp.tanh(u)
                        bent = u * t
                        steep = t + u * (1.0 - t * t)
                        one = jnp.where(row_of == r, weights, jnp.zeros_like(weights))
                        total = total + dot(
                            one[:, :size], jnp.concatenate([bent, steep], axis=1)
                        )
                    aggregate_ref[target, here, :] += total[:, :width]
                    pair_sum_ref[here, :] += total[:, width:]
                    return 0

                lax.fori_loop(0, blocks(live_target), block, 0)

            over_sizes(live_source, visit)
            slope_ref[target] += pair_sum_ref[...]
            slope_shift_ref[target] += alpha * pair_sum_ref[...]

        return 0

    lax.fori_loop(0, listed, forward_pair, 0)

    latent = latent_ref[0, 0].reshape(rows, width)
    agg_b = aggregate_ref[...].reshape(rows, width).astype(BF)
    message = dot(agg_b, edge_out_ref[...]).astype(BF)
    hidden_pre = (
        dot(latent, node_in_ref[:width, :])
        + dot(message, node_in_ref[width:, :])
        + node_in_bias_ref[...]
    )
    gate = sigmoid(hidden_pre)
    hidden_b = (hidden_pre * gate).astype(BF)
    pre_norm = dot(hidden_b, node_out_ref[...]) + node_out_bias_ref[...]
    centred = pre_norm - jnp.mean(pre_norm, axis=-1, keepdims=True)
    inverse = lax.rsqrt(jnp.mean(centred * centred, axis=-1, keepdims=True) + 1e-05)
    normed = centred * inverse
    gain = gain_ref[...]
    new_rows = (latent.astype(F32) + normed * gain).astype(BF)
    new_latent_ref[0, 0] = new_rows.reshape(cells, particles, width)

    cotangent = cotangent_ref[0, 0].reshape(rows, width).astype(F32)
    gain_sum = column_sum(cotangent * normed)
    scaled = cotangent * gain
    grad_pre = inverse * (
        scaled
        - jnp.mean(scaled, axis=-1, keepdims=True)
        - normed * jnp.mean(scaled * normed, axis=-1, keepdims=True)
    )
    grad_pre_b = grad_pre.astype(BF)
    out_bias_sum = column_sum(grad_pre)
    pack_ref[640:768, :] = t_dot(hidden_b, grad_pre_b).astype(BF)
    grad_hidden = dot_t(grad_pre_b, node_out_ref[...]) * (
        gate * (1.0 + hidden_pre * (1.0 - gate))
    )
    grad_hidden_b = grad_hidden.astype(BF)
    in_bias_sum = column_sum(grad_hidden)
    pack_ref[384:512, :] = t_dot(latent, grad_hidden_b).astype(BF)
    pack_ref[512:640, :] = t_dot(message, grad_hidden_b).astype(BF)
    grad_message = dot_t(grad_hidden_b, node_in_ref[width:, :]).astype(BF)
    pack_ref[256:384, :] = t_dot(agg_b, grad_message).astype(BF)
    upstream = dot_t(grad_message, edge_out_ref[...])
    upstream_ref[...] = upstream.reshape(cells, particles, width)
    grad_rows = cotangent + dot_t(grad_hidden_b, node_in_ref[:width, :])
    latent_grad_ref[0, 0] = grad_rows.reshape(cells, particles, width)

    def backward_pair(slot, _):
        target, source, _, alpha, beta = pair_of(slot)
        live_target = live_ref[target + 1]
        live_source = live_ref[source]

        @pl.when(live_source > 0)
        def _():
            set_pair(target, source, alpha, beta)
            pair_sum_ref[...] = dot(weight_t_ref[slot], upstream_ref[target].astype(BF))

            def visit(size):
                def block(index, _):
                    first = pl.multiple_of(index * GRAIN, GRAIN)
                    here = pl.ds(first, GRAIN)
                    weights = weight_t_ref[slot, here, :][:, :size]
                    a = a_half_ref[0:size, :]
                    up = upstream_ref[target, 0:size, :].astype(BF)

                    def steep(r):
                        b = b_ref[pl.ds(first + r, 1), :].astype(BF)
                        u = jnp.broadcast_to(b, (size, width)) + a
                        t = jnp.tanh(u)
                        return up * (t + u * (1.0 - t * t))

                    total = jnp.zeros((GRAIN, width), F32)
                    for r in range(0, GRAIN, 2):
                        both = dot(weights, jnp.concatenate([steep(r), steep(r + 1)], axis=1))
                        total = jnp.where(row_of == r, both[:, :width], total)
                        total = jnp.where(row_of == r + 1, both[:, width:], total)
                    pair_sum_ref[here, :] += total
                    return 0

                lax.fori_loop(0, blocks(live_source), block, 0)

            over_sizes(live_target, visit)
            grads = 0.5 * pair_sum_ref[...]
            source_grad_ref[source] += grads
            shift_ref[...] += beta * jnp.sum(grads.reshape(particles // 8, 8, width), axis=0)

        return 0

    lax.fori_loop(0, listed, backward_pair, 0)

    upstream = upstream_ref[...].reshape(rows, width)
    target_grad = 0.5 * upstream * slope_ref[...].reshape(rows, width)
    target_b = target_grad.astype(BF)
    source_grad = source_grad_ref[...].reshape(rows + 2 * particles, width)
    source_b = source_grad.astype(BF)
    own_b = source_b[particles : particles + rows]
    rim_grad_ref[0] = source_b[:particles]
    rim_grad_ref[1] = source_b[particles + rows :]
    latent = latent_ref[0, 0].reshape(rows, width)
    pack_ref[0:128, :] = t_dot(latent, target_b).astype(BF)
    pack_ref[128:256, :] = (
        t_dot(latent, own_b)
        + t_dot(before_ref[:particles, :], source_b[:particles])
        + t_dot(after_ref[:particles, :], source_b[particles + rows :])
    ).astype(BF)
    more = dot_t(target_b, target_w_ref[...]) + dot_t(own_b, source_w_ref[...])
    latent_grad_ref[0, 0] += more.reshape(cells, particles, width)
    x_target = x_ref[1 : cells + 1].reshape(rows, width)
    y_target = y_ref[1 : cells + 1].reshape(rows, width)
    x_source = x_ref[...].reshape(rows + 2 * particles, width)
    y_source = y_ref[...].reshape(rows + 2 * particles, width)
    shift = 0.5 * upstream * slope_shift_ref[...].reshape(rows, width)
    along = (
        column_sum(x_target * target_grad + shift)
        - column_sum(x_source * source_grad)
        + column_sum(shift_ref[...])
    )
    across = column_sum((y_target - 0.5) * target_grad) - column_sum((y_source - 0.5) * source_grad)
    small = jnp.concatenate(
        [
            along,
            across,
            column_sum(target_grad),
            in_bias_sum,
            out_bias_sum,
            gain_sum,
            jnp.zeros((2, width), F32),
        ],
        axis=0,
    )
    coarse = small.astype(BF).astype(F32)
    pack_ref[768:784, :] = jnp.concatenate([coarse, small - coarse], axis=0).astype(BF)
    pack_ref[784:800, :] = jnp.zeros((16, width), BF)


def run_step(scalars, arrays, latent, cells, particles, width):
    vmem = pl.BlockSpec(memory_space=pltpu.VMEM)
    smem = pl.BlockSpec(memory_space=pltpu.SMEM)
    window = cells + 2
    tile = (particles, width)
    pairs = scalars[1].shape[-1]
    return pl.pallas_call(
        step_kernel,
        in_specs=[smem] * len(scalars) + [vmem] * len(arrays),
        out_specs=[vmem] * 4,
        out_shape=[
            jax.ShapeDtypeStruct(latent.shape, BF),
            jax.ShapeDtypeStruct(latent.shape, F32),
            jax.ShapeDtypeStruct((2,) + tile, BF),
            jax.ShapeDtypeStruct((PACK_ROWS, width), BF),
        ],
        scratch_shapes=[
            pltpu.SMEM((window,), jnp.int32),
            pltpu.VMEM((window, META, particles), F32),
            pltpu.VMEM((window,) + tile, F32),
            pltpu.VMEM((window,) + tile, F32),
            pltpu.VMEM((cells,) + tile, F32),
            pltpu.VMEM((window,) + tile, F32),
            pltpu.VMEM((pairs, particles, particles), BF),
            pltpu.VMEM((pairs, particles, particles), BF),
            pltpu.VMEM((cells,) + tile, F32),
            pltpu.VMEM((cells,) + tile, F32),
            pltpu.VMEM((cells,) + tile, F32),
            pltpu.VMEM((cells,) + tile, F32),
            pltpu.VMEM((window,) + tile, F32),
            pltpu.VMEM(tile, F32),
            pltpu.VMEM(tile, BF),
            pltpu.VMEM(tile, F32),
            pltpu.VMEM(tile, BF),
            pltpu.VMEM(tile, F32),
            pltpu.VMEM((8, width), F32),
        ],
        compiler_params=pltpu.CompilerParams(vmem_limit_bytes=40 << 20),
        name="step",
    )(*scalars, *arrays)


def finish_kernel(
    core_ref,
    mine_ref,
    other_ref,
    partial_ref,
    rims_ref,
    source_w_ref,
    latent_grad_ref,
    target_w_out,
    source_w_out,
    offset_out,
    bias_out,
    edge_out_out,
    node_in_out,
    in_bias_out,
    node_out_out,
    out_bias_out,
    gain_out,
    *,
    scale,
):
    cells = partial_ref.shape[2]
    mine = mine_ref[...].astype(F32)
    other = other_ref[...].astype(F32)
    first = core_ref[0] == 0
    low = jnp.where(first, mine, other) * scale
    high = jnp.where(first, other, mine) * scale
    whole = jnp.concatenate([low, high], axis=0)
    target_w_out[...] = whole[0:128]
    source_w_out[...] = whole[128:256]
    edge_out_out[...] = whole[256:384]
    node_in_out[...] = whole[384:640]
    node_out_out[...] = whole[640:768]
    small = whole[768:776] + whole[776:784]
    offset_out[...] = small[0:2]
    bias_out[...] = small[2:3]
    in_bias_out[...] = small[3:4]
    out_bias_out[...] = small[4:5]
    gain_out[...] = small[5:6]
    latent_grad_ref[...] = partial_ref[...]
    latent_grad_ref[0, 0, cells - 1] += dot_t(rims_ref[0], source_w_ref[...])
    latent_grad_ref[0, 0, 0] += dot_t(rims_ref[1], source_w_ref[...])


def run_finish(core, mine, other, partial, rims, source_w, scale):
    width = mine.shape[-1]
    vmem = pl.BlockSpec(memory_space=pltpu.VMEM)
    smem = pl.BlockSpec(memory_space=pltpu.SMEM)
    square = jax.ShapeDtypeStruct((width, width), F32)
    row = jax.ShapeDtypeStruct((1, width), F32)
    return pl.pallas_call(
        functools.partial(finish_kernel, scale=scale),
        in_specs=[smem] + [vmem] * 5,
        out_specs=[vmem] * 11,
        out_shape=[
            jax.ShapeDtypeStruct(partial.shape, F32),
            square,
            square,
            jax.ShapeDtypeStruct((2, width), F32),
            row,
            square,
            jax.ShapeDtypeStruct((2 * width, width), F32),
            row,
            square,
            row,
            row,
        ],
        compiler_params=pltpu.CompilerParams(vmem_limit_bytes=32 << 20),
        name="finish",
    )(core, mine, other, partial, rims, source_w)


def neighbours(axis, by):
    length = lax.axis_size(axis)
    return [(i, i + by) for i in range(length) if 0 <= i + by < length]


def swap_cores(array):
    size = lax.axis_size("wide")
    return lax.ppermute(array, "wide", [(i, i ^ 1) for i in range(size)])


def exchange(array, axis, groups=None):
    return lax.all_to_all(array, axis, 0, 0, axis_index_groups=groups, tiled=True)


def spread(array, count):
    return jnp.broadcast_to(array[None], (count,) + array.shape)


def sum_everywhere(pack, core):
    width = pack.shape[-1]
    space = lax.axis_size("space")
    wide = lax.axis_size("wide")
    fellows = [list(range(start, wide, 2)) for start in range(2)]
    halves = pack.reshape(2, -1, width)
    mine = jnp.where(core == 0, halves[0], halves[1])
    sent = jnp.where(core == 0, halves[1], halves[0])
    half = mine.astype(F32) + swap_cores(sent).astype(F32)
    parts = half.astype(BF).reshape(space, -1, width)
    part = jnp.sum(exchange(parts, "space").astype(F32), axis=0).astype(BF)
    others = exchange(spread(part, wide // 2), "wide", fellows)
    part = jnp.sum(others.astype(F32), axis=0).astype(BF)
    return exchange(spread(part, space), "space").reshape(-1, width)


def on_device(
    latent,
    coords,
    cell_counts,
    pair_target,
    pair_source,
    pair_count,
    edge_target_w,
    edge_source_w,
    edge_offset,
    edge_bias,
    edge_out,
    node_in,
    node_in_bias,
    node_out,
    node_out_bias,
    norm_gain,
    cotangent,
):
    cells, particles, width = latent.shape[2:]
    core = lax.rem(lax.axis_index("wide"), 2)
    live = (
        jnp.arange(particles, dtype=jnp.int32)[None, :] < cell_counts[0, 0][:, None]
    ).astype(BF)
    meta = jnp.concatenate(
        [coords[0, 0], live[:, None, :], jnp.zeros((cells, META - 3, particles), BF)], axis=1
    )
    last = jnp.concatenate([latent[0, 0, cells - 1], meta[cells - 1]], axis=0)
    initial = jnp.concatenate([latent[0, 0, 0], meta[0]], axis=0)
    before = lax.ppermute(last, "space", neighbours("space", 1))
    after = lax.ppermute(initial, "space", neighbours("space", -1))
    new_rows, partial, rims, pack = run_step(
        (cell_counts, pair_target, pair_source, pair_count),
        (
            latent,
            meta,
            before,
            after,
            edge_target_w,
            edge_source_w,
            edge_offset,
            edge_bias[None, :],
            edge_out,
            node_in,
            node_in_bias[None, :],
            node_out,
            node_out_bias[None, :],
            norm_gain[None, :],
            cotangent,
        ),
        latent,
        cells,
        particles,
        width,
    )
    from_next = lax.ppermute(rims[0], "space", neighbours("space", -1))
    from_prev = lax.ppermute(rims[1], "space", neighbours("space", 1))
    mine = sum_everywhere(pack, core)
    other = swap_cores(mine)
    scale = 1.0 / math.sqrt(lax.axis_size("space") * lax.axis_size("wide") * cells * particles)
    rims_in = jnp.stack([from_next, from_prev])
    outs = run_finish(
        core.astype(jnp.int32)[None], mine, other, partial, rims_in, edge_source_w, scale
    )
    (latent_grad, target_w, source_w, offset, bias, out_w, in_w, in_bias, node_w, out_bias, gain) = outs
    return (
        new_rows,
        latent_grad,
        target_w,
        source_w,
        offset,
        bias[0],
        out_w,
        in_w,
        in_bias[0],
        node_w,
        out_bias[0],
        gain[0],
    )


def solution(mesh):
    cell = P("wide", "space", None, None, None)
    table = P("wide", "space", None)
    return jax.shard_map(
        on_device,
        mesh=mesh,
        in_specs=(cell, cell, table, table, table, P("wide", "space")) + (P(),) * 10 + (cell,),
        out_specs=(cell, cell) + (P(),) * 10,
        check_vma=False,
    )
```

```python
import functools
import math

import jax
import jax.numpy as jnp
from jax import lax
from jax.experimental import pallas as pl
from jax.experimental.pallas import tpu as pltpu
from jax.sharding import PartitionSpec as P

BF = jnp.bfloat16
F32 = jnp.float32
META = 16
GRAIN = 16
STEP = 16
ROWS = 64
PACK_ROWS = 800


def dot(a, b):
    return jnp.dot(a, b, preferred_element_type=F32)


def dot_t(a, b):
    return lax.dot_general(a, b, (((1,), (1,)), ((), ())), preferred_element_type=F32)


def t_dot(a, b):
    return lax.dot_general(a, b, (((0,), (0,)), ((), ())), preferred_element_type=F32)


def sigmoid(v):
    return 0.5 * (1.0 + jnp.tanh(0.5 * v))


def blocks(count, rows):
    return lax.div(count + (rows - 1), rows)


def column_sum(values):
    return jnp.sum(values, axis=0, keepdims=True)


def step_kernel(
    counts_ref,
    targets_ref,
    sources_ref,
    listed_ref,
    latent_ref,
    meta_ref,
    before_ref,
    after_ref,
    target_w_ref,
    source_w_ref,
    offset_ref,
    bias_ref,
    edge_out_ref,
    node_in_ref,
    node_in_bias_ref,
    node_out_ref,
    node_out_bias_ref,
    gain_ref,
    cotangent_ref,
    new_latent_ref,
    latent_grad_ref,
    rim_grad_ref,
    pack_ref,
    live_ref,
    place_ref,
    x_ref,
    y_ref,
    a_base_ref,
    b_base_ref,
    weight_ref,
    weight_t_ref,
    aggregate_ref,
    slope_ref,
    slope_shift_ref,
    upstream_ref,
    source_grad_ref,
    a_ref,
    a_half_ref,
    b_ref,
    b_half_ref,
    pair_sum_ref,
    shift_ref,
    order_ref,
    rows_ref,
    cotangent_rows_ref,
    bounds_ref,
    bounds_smem,
    bounds_sem,
):
    cells, particles, width = latent_ref.shape[2:]
    rows = cells * particles
    offset_x = offset_ref[0:1, :]
    offset_y = offset_ref[1:2, :]

    sub = lax.broadcasted_iota(jnp.int32, (particles, particles), 0)
    lane = lax.broadcasted_iota(jnp.int32, (particles, particles), 1)
    pick = lax.broadcasted_iota(jnp.int32, (META, width), 0)
    pick_x = jnp.where(pick == 0, 1.0, 0.0).astype(BF)
    pick_y = jnp.where(pick == 1, 1.0, 0.0).astype(BF)
    pick_key = jnp.where(pick == 3, 1.0, 0.0).astype(BF)
    for slot in range(cells + 2):
        if slot == 0:
            rows_in = before_ref[:particles, :]
            place = before_ref[particles:, :].astype(F32)
            live_ref[slot] = jnp.sum(place[2:3, :]).astype(jnp.int32)
        elif slot == cells + 1:
            rows_in = after_ref[:particles, :]
            place = after_ref[particles:, :].astype(F32)
            live_ref[slot] = jnp.sum(place[2:3, :]).astype(jnp.int32)
        else:
            rows_in = latent_ref[0, 0, slot - 1]
            place = meta_ref[slot - 1].astype(F32)
            live_ref[slot] = counts_ref[0, 0, slot - 1]
        key = jnp.where(place[2:3, :] > 0.5, place[0:1, :], 2.0)
        place = jnp.where(pick == 3, key, place).astype(BF)
        keys = t_dot(place, pick_key)
        ahead = (keys < key) | ((keys == key) & (sub < lane))
        rank = column_sum(jnp.where(ahead, 1.0, 0.0))
        order = jnp.where(sub.astype(F32) == rank, 1.0, 0.0).astype(BF)
        order_ref[slot] = order
        place = dot_t(place, order)
        place_ref[slot] = place
        place = place.astype(BF)
        x = t_dot(place, pick_x)
        y = t_dot(place, pick_y)
        x_ref[slot] = x
        y_ref[slot] = y
        moved = x * offset_x + (y - 0.5) * offset_y
        rows_in = dot(order, rows_in).astype(BF)
        rows_ref[slot] = rows_in
        proj_source = dot(rows_in, source_w_ref[...]).astype(BF).astype(F32)
        b_base_ref[slot] = 0.5 * (proj_source - moved)
        if 0 < slot < cells + 1:
            proj_target = (dot(rows_in, target_w_ref[...]) + bias_ref[...]).astype(BF)
            a_base_ref[slot - 1] = 0.5 * (proj_target.astype(F32) + moved)
            cotangent_rows_ref[slot - 1] = dot(order, cotangent_ref[0, 0, slot - 1]).astype(BF)

    aggregate_ref[...] = jnp.zeros_like(aggregate_ref)
    slope_ref[...] = jnp.zeros_like(slope_ref)
    slope_shift_ref[...] = jnp.zeros_like(slope_shift_ref)
    source_grad_ref[...] = jnp.zeros_like(source_grad_ref)
    shift_ref[...] = jnp.zeros_like(shift_ref)

    row_of = lax.broadcasted_iota(jnp.int32, (GRAIN, width), 0)
    listed = listed_ref[0, 0]

    def pair_of(slot):
        target = targets_ref[0, 0, slot]
        source = sources_ref[0, 0, slot]
        off = (target - source + 1).astype(F32)
        alpha = jnp.where(off < -0.5, -1.0, jnp.where(off > 0.5, 0.0, -0.5))
        return target, source, off, alpha, off - alpha

    def set_pair(target, source, alpha, beta):
        a = a_base_ref[target] + (0.5 * alpha) * offset_x
        b = b_base_ref[source] + (0.5 * beta) * offset_x
        a_ref[...] = a
        b_ref[...] = b
        a_half_ref[...] = a.astype(BF)
        b_half_ref[...] = b.astype(BF)

    def bound_pair(slot, _):
        target, source, off, _, _ = pair_of(slot)
        live_target = live_ref[target + 1]
        live_source = live_ref[source]

        def counted(hit):
            return column_sum(jnp.where(hit, 1.0, 0.0)).astype(jnp.int32)

        x_target, row_target = x_ref[target + 1], place_ref[target + 1, 0:1, :]
        x_source, row_source = x_ref[source], place_ref[source, 0:1, :]
        zero = jnp.zeros((1, particles), jnp.int32)
        source_at_most = counted((x_source <= row_target) & (sub < live_source))
        source_below = counted((x_source < row_target) & (sub < live_source))
        target_at_most = counted((x_target <= row_source) & (sub < live_target))
        target_below = counted((x_target < row_source) & (sub < live_target))
        bounds_ref[slot] = jnp.concatenate(
            [
                jnp.where(off > 0.5, source_at_most, zero),
                jnp.where(off < -0.5, source_below, zero + live_source),
                jnp.where(off < -0.5, target_at_most, zero),
                jnp.where(off > 0.5, target_below, zero + live_target),
                jnp.zeros((4, particles), jnp.int32),
            ],
            axis=0,
        )
        return 0

    lax.fori_loop(0, listed, bound_pair, 0)
    bounds_copy = pltpu.make_async_copy(bounds_ref, bounds_smem, bounds_sem)
    bounds_copy.start()
    bounds_copy.wait()

    def over_range(slot, which, first, live, visit):
        last = jnp.minimum(first + (ROWS - 1), live - 1)
        start = lax.div(bounds_smem[slot, which, first], STEP)
        most = particles // STEP
        size = jnp.clip(blocks(bounds_smem[slot, which + 1, last], STEP) - start, 0, most)
        lax.switch(
            size,
            [lambda at: None]
            + [functools.partial(visit, STEP * count) for count in range(1, most + 1)],
            jnp.clip(start, 0, most - size) * STEP,
        )

    def forward_pair(slot, _):
        target, source, off, alpha, beta = pair_of(slot)
        live_target = live_ref[target + 1]
        live_source = live_ref[source]

        @pl.when(live_source > 0)
        def _():
            set_pair(target, source, alpha, beta)
            dx = (off + x_ref[target + 1]) - place_ref[source, 0:1, :]
            dy = y_ref[target + 1] - place_ref[source, 1:2, :]
            near = jnp.maximum(1.0 - dx * dx - dy * dy, 0.0)
            keep = (sub < live_target) & (lane < live_source)
            weight = jnp.where(keep, near * near, 0.0).astype(BF)
            weight_ref[slot] = weight
            dx = (off + place_ref[target + 1, 0:1, :]) - x_ref[source]
            dy = place_ref[target + 1, 1:2, :] - y_ref[source]
            near = jnp.maximum(1.0 - dx * dx - dy * dy, 0.0)
            keep = (lane < live_target) & (sub < live_source)
            weight_t_ref[slot] = jnp.where(keep, near * near, 0.0).astype(BF)
            ones = jnp.ones((particles, width), BF)
            linear = dot(weight, jnp.concatenate([b_half_ref[...], ones], axis=1))
            weight_sum = linear[:, width:]
            aggregate_ref[target] += a_ref[...] * weight_sum + linear[:, :width]
            pair_sum_ref[...] = weight_sum

            def block(index, _):
                first = pl.multiple_of(index * ROWS, ROWS)

                def visit(size, at):
                    at = pl.multiple_of(at, STEP)
                    b = b_half_ref[pl.ds(at, size), :]
                    for group in range(0, ROWS, GRAIN):
                        here = pl.ds(first + group, GRAIN)
                        weights = weight_ref[slot, here, :].astype(F32)
                        weights = pltpu.roll(weights, particles - at, axis=1).astype(BF)
                        total = jnp.zeros((GRAIN, 2 * width), F32)
                        for r in range(GRAIN):
                            a = a_ref[pl.ds(first + group + r, 1), :].astype(BF)
                            u = jnp.broadcast_to(a, (size, width)) + b
                            t = jnp.tanh(u)
                            bent = u * t
                            steep = t + u * (1.0 - t * t)
                            one = jnp.where(row_of == r, weights, jnp.zeros_like(weights))
                            total = total + dot(
                                one[:, :size], jnp.concatenate([bent, steep], axis=1)
                            )
                        aggregate_ref[target, here, :] += total[:, :width]
                        pair_sum_ref[here, :] += total[:, width:]

                over_range(slot, 0, first, live_target, visit)
                return 0

            lax.fori_loop(0, blocks(live_target, ROWS), block, 0)
            slope_ref[target] += pair_sum_ref[...]
            slope_shift_ref[target] += alpha * pair_sum_ref[...]

        return 0

    lax.fori_loop(0, listed, forward_pair, 0)

    latent = rows_ref[1 : cells + 1].reshape(rows, width)
    agg_b = aggregate_ref[...].reshape(rows, width).astype(BF)
    message = dot(agg_b, edge_out_ref[...]).astype(BF)
    hidden_pre = (
        dot(latent, node_in_ref[:width, :])
        + dot(message, node_in_ref[width:, :])
        + node_in_bias_ref[...]
    )
    gate = sigmoid(hidden_pre)
    hidden_b = (hidden_pre * gate).astype(BF)
    pre_norm = dot(hidden_b, node_out_ref[...]) + node_out_bias_ref[...]
    centred = pre_norm - jnp.mean(pre_norm, axis=-1, keepdims=True)
    inverse = lax.rsqrt(jnp.mean(centred * centred, axis=-1, keepdims=True) + 1e-05)
    normed = centred * inverse
    gain = gain_ref[...]
    new_rows = (latent.astype(F32) + normed * gain).astype(BF)
    for cell in range(cells):
        there = new_rows[cell * particles : (cell + 1) * particles]
        new_latent_ref[0, 0, cell] = t_dot(order_ref[cell + 1], there).astype(BF)

    cotangent = cotangent_rows_ref[...].reshape(rows, width).astype(F32)
    gain_sum = column_sum(cotangent * normed)
    scaled = cotangent * gain
    grad_pre = inverse * (
        scaled
        - jnp.mean(scaled, axis=-1, keepdims=True)
        - normed * jnp.mean(scaled * normed, axis=-1, keepdims=True)
    )
    grad_pre_b = grad_pre.astype(BF)
    out_bias_sum = column_sum(grad_pre)
    pack_ref[640:768, :] = t_dot(hidden_b, grad_pre_b).astype(BF)
    grad_hidden = dot_t(grad_pre_b, node_out_ref[...]) * (
        gate * (1.0 + hidden_pre * (1.0 - gate))
    )
    grad_hidden_b = grad_hidden.astype(BF)
    in_bias_sum = column_sum(grad_hidden)
    pack_ref[384:512, :] = t_dot(latent, grad_hidden_b).astype(BF)
    pack_ref[512:640, :] = t_dot(message, grad_hidden_b).astype(BF)
    grad_message = dot_t(grad_hidden_b, node_in_ref[width:, :]).astype(BF)
    pack_ref[256:384, :] = t_dot(agg_b, grad_message).astype(BF)
    upstream = dot_t(grad_message, edge_out_ref[...])
    upstream_ref[...] = upstream.reshape(cells, particles, width)
    grad_rows = cotangent + dot_t(grad_hidden_b, node_in_ref[:width, :])
    aggregate_ref[...] = grad_rows.reshape(cells, particles, width)

    def backward_pair(slot, _):
        target, source, _, alpha, beta = pair_of(slot)
        live_target = live_ref[target + 1]
        live_source = live_ref[source]

        @pl.when(live_source > 0)
        def _():
            set_pair(target, source, alpha, beta)
            pair_sum_ref[...] = dot(weight_t_ref[slot], upstream_ref[target].astype(BF))

            def block(index, _):
                first = pl.multiple_of(index * ROWS, ROWS)

                def visit(size, at):
                    at = pl.multiple_of(at, STEP)
                    a = a_half_ref[pl.ds(at, size), :]
                    up = upstream_ref[target, pl.ds(at, size), :].astype(BF)

                    def steep(row):
                        b = b_ref[pl.ds(first + row, 1), :].astype(BF)
                        u = jnp.broadcast_to(b, (size, width)) + a
                        t = jnp.tanh(u)
                        return up * (t + u * (1.0 - t * t))

                    for group in range(0, ROWS, GRAIN):
                        here = pl.ds(first + group, GRAIN)
                        weights = weight_t_ref[slot, here, :].astype(F32)
                        weights = pltpu.roll(weights, particles - at, axis=1).astype(BF)
                        total = jnp.zeros((GRAIN, width), F32)
                        for r in range(0, GRAIN, 2):
                            pair = jnp.concatenate([steep(group + r), steep(group + r + 1)], axis=1)
                            both = dot(weights[:, :size], pair)
                            total = jnp.where(row_of == r, both[:, :width], total)
                            total = jnp.where(row_of == r + 1, both[:, width:], total)
                        pair_sum_ref[here, :] += total

                over_range(slot, 2, first, live_source, visit)
                return 0

            lax.fori_loop(0, blocks(live_source, ROWS), block, 0)
            grads = 0.5 * pair_sum_ref[...]
            source_grad_ref[source] += grads
            shift_ref[...] += beta * jnp.sum(grads.reshape(particles // 8, 8, width), axis=0)

        return 0

    lax.fori_loop(0, listed, backward_pair, 0)

    upstream = upstream_ref[...].reshape(rows, width)
    target_grad = 0.5 * upstream * slope_ref[...].reshape(rows, width)
    target_b = target_grad.astype(BF)
    source_grad = source_grad_ref[...].reshape(rows + 2 * particles, width)
    source_b = source_grad.astype(BF)
    own_b = source_b[particles : particles + rows]
    rim_grad_ref[0] = t_dot(order_ref[0], source_b[:particles]).astype(BF)
    rim_grad_ref[1] = t_dot(order_ref[cells + 1], source_b[particles + rows :]).astype(BF)
    latent = rows_ref[1 : cells + 1].reshape(rows, width)
    pack_ref[0:128, :] = t_dot(latent, target_b).astype(BF)
    pack_ref[128:256, :] = (
        t_dot(latent, own_b)
        + t_dot(rows_ref[0], source_b[:particles])
        + t_dot(rows_ref[cells + 1], source_b[particles + rows :])
    ).astype(BF)
    more = dot_t(target_b, target_w_ref[...]) + dot_t(own_b, source_w_ref[...])
    grad_rows = aggregate_ref[...].reshape(rows, width) + more
    for cell in range(cells):
        there = grad_rows[cell * particles : (cell + 1) * particles]
        coarse = there.astype(BF)
        fine = (there - coarse.astype(F32)).astype(BF)
        both = t_dot(order_ref[cell + 1], jnp.concatenate([coarse, fine], axis=1))
        latent_grad_ref[0, 0, cell] = both[:, :width] + both[:, width:]
    x_target = x_ref[1 : cells + 1].reshape(rows, width)
    y_target = y_ref[1 : cells + 1].reshape(rows, width)
    x_source = x_ref[...].reshape(rows + 2 * particles, width)
    y_source = y_ref[...].reshape(rows + 2 * particles, width)
    shift = 0.5 * upstream * slope_shift_ref[...].reshape(rows, width)
    along = (
        column_sum(x_target * target_grad + shift)
        - column_sum(x_source * source_grad)
        + column_sum(shift_ref[...])
    )
    across = column_sum((y_target - 0.5) * target_grad) - column_sum((y_source - 0.5) * source_grad)
    small = jnp.concatenate(
        [
            along,
            across,
            column_sum(target_grad),
            in_bias_sum,
            out_bias_sum,
            gain_sum,
            jnp.zeros((2, width), F32),
        ],
        axis=0,
    )
    coarse = small.astype(BF).astype(F32)
    pack_ref[768:784, :] = jnp.concatenate([coarse, small - coarse], axis=0).astype(BF)
    pack_ref[784:800, :] = jnp.zeros((16, width), BF)


def whole(array):
    return pl.BlockSpec(array.shape, lambda step: (0,) * len(array.shape))


def run_step(scalars, arrays, latent, cells, particles, width):
    smem = pl.BlockSpec(memory_space=pltpu.SMEM)
    window = cells + 2
    tile = (particles, width)
    pairs = scalars[1].shape[-1]
    outs = [
        jax.ShapeDtypeStruct(latent.shape, BF),
        jax.ShapeDtypeStruct(latent.shape, F32),
        jax.ShapeDtypeStruct((2,) + tile, BF),
        jax.ShapeDtypeStruct((PACK_ROWS, width), BF),
    ]
    return pl.pallas_call(
        step_kernel,
        grid=(1,),
        in_specs=[smem] * len(scalars) + [whole(array) for array in arrays],
        out_specs=[whole(array) for array in outs],
        out_shape=outs,
        scratch_shapes=[
            pltpu.SMEM((window,), jnp.int32),
            pltpu.VMEM((window, META, particles), F32),
            pltpu.VMEM((window,) + tile, F32),
            pltpu.VMEM((window,) + tile, F32),
            pltpu.VMEM((cells,) + tile, F32),
            pltpu.VMEM((window,) + tile, F32),
            pltpu.VMEM((pairs, particles, particles), BF),
            pltpu.VMEM((pairs, particles, particles), BF),
            pltpu.VMEM((cells,) + tile, F32),
            pltpu.VMEM((cells,) + tile, F32),
            pltpu.VMEM((cells,) + tile, F32),
            pltpu.VMEM((cells,) + tile, F32),
            pltpu.VMEM((window,) + tile, F32),
            pltpu.VMEM(tile, F32),
            pltpu.VMEM(tile, BF),
            pltpu.VMEM(tile, F32),
            pltpu.VMEM(tile, BF),
            pltpu.VMEM(tile, F32),
            pltpu.VMEM((8, width), F32),
            pltpu.VMEM((window,) + tile, BF),
            pltpu.VMEM((window,) + tile, BF),
            pltpu.VMEM((cells,) + tile, BF),
            pltpu.VMEM((pairs, 8, particles), jnp.int32),
            pltpu.SMEM((pairs, 8, particles), jnp.int32),
            pltpu.SemaphoreType.DMA,
        ],
        compiler_params=pltpu.CompilerParams(vmem_limit_bytes=56 << 20),
        name="step",
    )(*scalars, *arrays)


def finish_kernel(
    core_ref,
    mine_ref,
    other_ref,
    partial_ref,
    rims_ref,
    source_w_ref,
    latent_grad_ref,
    target_w_out,
    source_w_out,
    offset_out,
    bias_out,
    edge_out_out,
    node_in_out,
    in_bias_out,
    node_out_out,
    out_bias_out,
    gain_out,
    *,
    scale,
):
    cells = partial_ref.shape[2]
    mine = mine_ref[...].astype(F32)
    other = other_ref[...].astype(F32)
    first = core_ref[0] == 0
    low = jnp.where(first, mine, other) * scale
    high = jnp.where(first, other, mine) * scale
    whole = jnp.concatenate([low, high], axis=0)
    target_w_out[...] = whole[0:128]
    source_w_out[...] = whole[128:256]
    edge_out_out[...] = whole[256:384]
    node_in_out[...] = whole[384:640]
    node_out_out[...] = whole[640:768]
    small = whole[768:776] + whole[776:784]
    offset_out[...] = small[0:2]
    bias_out[...] = small[2:3]
    in_bias_out[...] = small[3:4]
    out_bias_out[...] = small[4:5]
    gain_out[...] = small[5:6]
    latent_grad_ref[...] = partial_ref[...]
    latent_grad_ref[0, 0, cells - 1] += dot_t(rims_ref[0], source_w_ref[...])
    latent_grad_ref[0, 0, 0] += dot_t(rims_ref[1], source_w_ref[...])


def run_finish(core, mine, other, partial, rims, source_w, scale):
    width = mine.shape[-1]
    vmem = pl.BlockSpec(memory_space=pltpu.VMEM)
    smem = pl.BlockSpec(memory_space=pltpu.SMEM)
    square = jax.ShapeDtypeStruct((width, width), F32)
    row = jax.ShapeDtypeStruct((1, width), F32)
    return pl.pallas_call(
        functools.partial(finish_kernel, scale=scale),
        in_specs=[smem] + [vmem] * 5,
        out_specs=[vmem] * 11,
        out_shape=[
            jax.ShapeDtypeStruct(partial.shape, F32),
            square,
            square,
            jax.ShapeDtypeStruct((2, width), F32),
            row,
            square,
            jax.ShapeDtypeStruct((2 * width, width), F32),
            row,
            square,
            row,
            row,
        ],
        compiler_params=pltpu.CompilerParams(vmem_limit_bytes=32 << 20),
        name="finish",
    )(core, mine, other, partial, rims, source_w)


def neighbours(axis, by):
    length = lax.axis_size(axis)
    return [(i, i + by) for i in range(length) if 0 <= i + by < length]


def swap_cores(array):
    size = lax.axis_size("wide")
    return lax.ppermute(array, "wide", [(i, i ^ 1) for i in range(size)])


def exchange(array, axis, groups=None):
    return lax.all_to_all(array, axis, 0, 0, axis_index_groups=groups, tiled=True)


def spread(array, count):
    return jnp.broadcast_to(array[None], (count,) + array.shape)


def sum_everywhere(pack, core):
    width = pack.shape[-1]
    space = lax.axis_size("space")
    wide = lax.axis_size("wide")
    fellows = [list(range(start, wide, 2)) for start in range(2)]
    halves = pack.reshape(2, -1, width)
    mine = jnp.where(core == 0, halves[0], halves[1])
    sent = jnp.where(core == 0, halves[1], halves[0])
    half = mine.astype(F32) + swap_cores(sent).astype(F32)
    parts = half.astype(BF).reshape(space, -1, width)
    part = jnp.sum(exchange(parts, "space").astype(F32), axis=0).astype(BF)
    others = exchange(spread(part, wide // 2), "wide", fellows)
    part = jnp.sum(others.astype(F32), axis=0).astype(BF)
    return exchange(spread(part, space), "space").reshape(-1, width)


def on_device(
    latent,
    coords,
    cell_counts,
    pair_target,
    pair_source,
    pair_count,
    edge_target_w,
    edge_source_w,
    edge_offset,
    edge_bias,
    edge_out,
    node_in,
    node_in_bias,
    node_out,
    node_out_bias,
    norm_gain,
    cotangent,
):
    cells, particles, width = latent.shape[2:]
    core = lax.rem(lax.axis_index("wide"), 2)
    live = (
        jnp.arange(particles, dtype=jnp.int32)[None, :] < cell_counts[0, 0][:, None]
    ).astype(BF)
    meta = jnp.concatenate(
        [coords[0, 0], live[:, None, :], jnp.zeros((cells, META - 3, particles), BF)], axis=1
    )
    last = jnp.concatenate([latent[0, 0, cells - 1], meta[cells - 1]], axis=0)
    initial = jnp.concatenate([latent[0, 0, 0], meta[0]], axis=0)
    before = lax.ppermute(last, "space", neighbours("space", 1))
    after = lax.ppermute(initial, "space", neighbours("space", -1))
    new_rows, partial, rims, pack = run_step(
        (cell_counts, pair_target, pair_source, pair_count),
        (
            latent,
            meta,
            before,
            after,
            edge_target_w,
            edge_source_w,
            edge_offset,
            edge_bias[None, :],
            edge_out,
            node_in,
            node_in_bias[None, :],
            node_out,
            node_out_bias[None, :],
            norm_gain[None, :],
            cotangent,
        ),
        latent,
        cells,
        particles,
        width,
    )
    from_next = lax.ppermute(rims[0], "space", neighbours("space", -1))
    from_prev = lax.ppermute(rims[1], "space", neighbours("space", 1))
    mine = sum_everywhere(pack, core)
    other = swap_cores(mine)
    scale = 1.0 / math.sqrt(lax.axis_size("space") * lax.axis_size("wide") * cells * particles)
    rims_in = jnp.stack([from_next, from_prev])
    outs = run_finish(
        core.astype(jnp.int32)[None], mine, other, partial, rims_in, edge_source_w, scale
    )
    (latent_grad, target_w, source_w, offset, bias, out_w, in_w, in_bias, node_w, out_bias, gain) = outs
    return (
        new_rows,
        latent_grad,
        target_w,
        source_w,
        offset,
        bias[0],
        out_w,
        in_w,
        in_bias[0],
        node_w,
        out_bias[0],
        gain[0],
    )


def solution(mesh):
    cell = P("wide", "space", None, None, None)
    table = P("wide", "space", None)
    return jax.shard_map(
        on_device,
        mesh=mesh,
        in_specs=(cell, cell, table, table, table, P("wide", "space")) + (P(),) * 10 + (cell,),
        out_specs=(cell, cell) + (P(),) * 10,
        check_vma=False,
    )
```

```python
import functools
import math
import types

import jax
import jax.numpy as jnp
from jax import lax
from jax.experimental import pallas as pl
from jax.experimental.pallas import tpu as pltpu
from jax.sharding import PartitionSpec as P

BF = jnp.bfloat16
F32 = jnp.float32
META = 16
GRAIN = 16
STEP = 16
ROWS = 64
PACK_ROWS = 800


def dot(a, b):
    return jnp.dot(a, b, preferred_element_type=F32)


def dot_t(a, b):
    return lax.dot_general(a, b, (((1,), (1,)), ((), ())), preferred_element_type=F32)


def t_dot(a, b):
    return lax.dot_general(a, b, (((0,), (0,)), ((), ())), preferred_element_type=F32)


def sigmoid(v):
    return 0.5 * (1.0 + jnp.tanh(0.5 * v))


def blocks(count, rows):
    return lax.div(count + (rows - 1), rows)


def column_sum(values):
    return jnp.sum(values, axis=0, keepdims=True)


def order_slot(s, slot, rows_in, place, target_w, bias):
    particles = place.shape[1]
    width = rows_in.shape[1]
    sub = lax.broadcasted_iota(jnp.int32, (particles, particles), 0)
    lane = lax.broadcasted_iota(jnp.int32, (particles, particles), 1)
    pick = lax.broadcasted_iota(jnp.int32, (META, width), 0)
    pick_key = jnp.where(pick == 3, 1.0, 0.0).astype(BF)
    key = jnp.where(place[2:3, :] > 0.5, place[0:1, :], 2.0)
    place = jnp.where(pick == 3, key, place).astype(BF)
    keys = t_dot(place, pick_key)
    ahead = (keys < key) | ((keys == key) & (sub < lane))
    rank = column_sum(jnp.where(ahead, 1.0, 0.0))
    order = jnp.where(sub.astype(F32) == rank, 1.0, 0.0).astype(BF)
    s.order[slot] = order
    s.place[slot] = dot_t(place, order)
    spread_place(s, slot)
    moved = s.x[slot] * s.offset[0:1, :] + (s.y[slot] - 0.5) * s.offset[1:2, :]
    rows_in = dot(order, rows_in).astype(BF)
    s.rows[slot] = rows_in
    proj_source = dot(rows_in, s.source_w[...]).astype(BF).astype(F32)
    s.b_base[slot] = 0.5 * (proj_source - moved)
    if target_w is not None:
        proj_target = (dot(rows_in, target_w[...]) + bias[...]).astype(BF)
        s.a_base[slot - 1] = 0.5 * (proj_target.astype(F32) + moved)


def spread_place(s, slot):
    pick = lax.broadcasted_iota(jnp.int32, s.place.shape[1:], 0)
    place = s.place[slot].astype(BF)
    s.x[slot] = t_dot(place, jnp.where(pick == 0, 1.0, 0.0).astype(BF))
    s.y[slot] = t_dot(place, jnp.where(pick == 1, 1.0, 0.0).astype(BF))


def pair_tools(s):
    particles, width = s.x.shape[1:]
    cells = s.a_base.shape[0]
    offset_x = s.offset[0:1, :]
    row_of = lax.broadcasted_iota(jnp.int32, (GRAIN, width), 0)
    sub = lax.broadcasted_iota(jnp.int32, (particles, particles), 0)
    listed = s.listed[0, 0]

    def pair_of(slot):
        target = s.targets[0, 0, slot]
        source = s.sources[0, 0, slot]
        off = (target - source + 1).astype(F32)
        alpha = jnp.where(off < -0.5, -1.0, jnp.where(off > 0.5, 0.0, -0.5))
        return target, source, off, alpha, off - alpha

    def bound_pair(slot, _):
        target, source, off, _, _ = pair_of(slot)
        live_target = s.live[target + 1]
        live_source = s.live[source]

        def counted(hit):
            return column_sum(jnp.where(hit, 1.0, 0.0)).astype(jnp.int32)

        x_target, row_target = s.x[target + 1], s.place[target + 1, 0:1, :]
        x_source, row_source = s.x[source], s.place[source, 0:1, :]
        zero = jnp.zeros((1, particles), jnp.int32)
        source_at_most = counted((x_source <= row_target) & (sub < live_source))
        source_below = counted((x_source < row_target) & (sub < live_source))
        target_at_most = counted((x_target <= row_source) & (sub < live_target))
        target_below = counted((x_target < row_source) & (sub < live_target))
        s.bounds[slot] = jnp.concatenate(
            [
                jnp.where(off > 0.5, source_at_most, zero),
                jnp.where(off < -0.5, source_below, zero + live_source),
                jnp.where(off < -0.5, target_at_most, zero),
                jnp.where(off > 0.5, target_below, zero + live_target),
                jnp.zeros((4, particles), jnp.int32),
            ],
            axis=0,
        )
        return 0

    def set_bounds():
        lax.fori_loop(0, listed, bound_pair, 0)
        copy = pltpu.make_async_copy(s.bounds, s.bounds_smem, s.bounds_sem)
        copy.start()
        copy.wait()

    def over_range(slot, which, first, live, visit):
        last = jnp.minimum(first + (ROWS - 1), live - 1)
        start = lax.div(s.bounds_smem[slot, which, first], STEP)
        most = particles // STEP
        size = jnp.clip(blocks(s.bounds_smem[slot, which + 1, last], STEP) - start, 0, most)
        lax.switch(
            size,
            [lambda at: None]
            + [functools.partial(visit, STEP * count) for count in range(1, most + 1)],
            jnp.clip(start, 0, most - size) * STEP,
        )

    lane_rows = lax.broadcasted_iota(jnp.int32, (GRAIN, particles), 1)

    def weights_of(x, y, there, at, first, live_here, live_there, shift):
        dx = (shift + x) - there[0:1, :]
        dy = y - there[1:2, :]
        near = jnp.maximum(1.0 - dx * dx - dy * dy, 0.0)
        keep = (row_of + first < live_here) & (lane_rows + at < live_there)
        return jnp.where(keep, near * near, 0.0).astype(BF)

    def forward_pair(slot, _):
        target, source, off, alpha, beta = pair_of(slot)
        live_target = s.live[target + 1]
        live_source = s.live[source]
        shift_a = (0.5 * alpha) * offset_x
        shift_b = (0.5 * beta) * offset_x

        def block(index, _):
            first = pl.multiple_of(index * ROWS, ROWS)

            def visit(size, at):
                at = pl.multiple_of(at, STEP)
                b = (s.b_base[source, pl.ds(at, size), :] + shift_b).astype(BF)
                there = pltpu.roll(s.place[source], particles - at, axis=1)
                for group in range(0, ROWS, GRAIN):
                    here = pl.ds(first + group, GRAIN)
                    x, y = s.x[target + 1, here, :], s.y[target + 1, here, :]
                    weights = weights_of(
                        x, y, there, at, first + group, live_target, live_source, off
                    )
                    total = jnp.zeros((GRAIN, 2 * width), F32)
                    for r in range(GRAIN):
                        a = s.a_base[target, pl.ds(first + group + r, 1), :] + shift_a
                        u = jnp.broadcast_to(a.astype(BF), (size, width)) + b
                        t = jnp.tanh(u)
                        bent = u + u * t
                        steep = 1.0 + (t + u * (1.0 - t * t))
                        one = jnp.where(row_of == r, weights, jnp.zeros_like(weights))
                        total = total + dot(
                            one[:, :size], jnp.concatenate([bent, steep], axis=1)
                        )
                    s.aggregate[target, here, :] += total[:, :width]
                    s.slope[target, here, :] += total[:, width:]
                    s.slope_shift[target, here, :] += alpha * total[:, width:]

            over_range(slot, 0, first, live_target, visit)
            return 0

        lax.fori_loop(0, blocks(live_target, ROWS), block, 0)
        return 0

    def forward(rim):
        def visit(slot, _):
            source = s.sources[0, 0, slot]
            at_rim = (source == 0) | (source == cells + 1)

            @pl.when(at_rim == rim)
            def _():
                forward_pair(slot, 0)

            return 0

        lax.fori_loop(0, listed, visit, 0)

    return pair_of, set_bounds, over_range, weights_of, forward


def own_kernel(
    counts,
    targets,
    sources,
    listed,
    latent_ref,
    meta_ref,
    target_w,
    source_w,
    offset,
    bias,
    place,
    order,
    rows,
    a_base,
    b_base,
    aggregate,
    slope,
    slope_shift,
    live,
    x,
    y,
    bounds,
    bounds_smem,
    bounds_sem,
):
    s = types.SimpleNamespace(**locals())
    cells = latent_ref.shape[2]
    live[0] = 0
    live[cells + 1] = 0
    for cell in range(cells):
        live[cell + 1] = counts[0, 0, cell]
        order_slot(
            s, cell + 1, latent_ref[0, 0, cell], meta_ref[cell].astype(F32), target_w, bias
        )
    for slot in (0, cells + 1):
        place[slot] = jnp.zeros(place.shape[1:], F32)
        order[slot] = jnp.zeros(order.shape[1:], BF)
        rows[slot] = jnp.zeros(rows.shape[1:], BF)
        b_base[slot] = jnp.zeros(b_base.shape[1:], F32)
        x[slot] = jnp.zeros(x.shape[1:], F32)
        y[slot] = jnp.zeros(y.shape[1:], F32)
    aggregate[...] = jnp.zeros_like(aggregate)
    slope[...] = jnp.zeros_like(slope)
    slope_shift[...] = jnp.zeros_like(slope_shift)
    _, set_bounds, _, _, forward = pair_tools(s)
    set_bounds()
    forward(False)


def step_kernel(
    counts,
    targets,
    sources,
    listed,
    before_ref,
    after_ref,
    cotangent_ref,
    place_in,
    order_in,
    rows_in,
    a_base,
    b_base_in,
    aggregate_in,
    slope_in,
    slope_shift_in,
    target_w,
    source_w,
    offset,
    edge_out_ref,
    node_in_ref,
    node_in_bias_ref,
    node_out_ref,
    node_out_bias_ref,
    gain_ref,
    new_latent_ref,
    latent_grad_ref,
    rim_grad_ref,
    pack_ref,
    live,
    place,
    order,
    rows,
    b_base,
    aggregate,
    slope,
    slope_shift,
    x,
    y,
    upstream_all,
    source_grad,
    shift,
    cotangent_rows,
    bounds,
    bounds_smem,
    bounds_sem,
):
    s = types.SimpleNamespace(**locals())
    s.upstream = upstream_all
    cells, particles, width = cotangent_ref.shape[2:]
    count = cells * particles
    row_of = lax.broadcasted_iota(jnp.int32, (GRAIN, width), 0)
    offset_x = offset[0:1, :]
    for cell in range(cells):
        slot = cell + 1
        live[slot] = counts[0, 0, cell]
        place[slot] = place_in[slot]
        order[slot] = order_in[slot]
        rows[slot] = rows_in[slot]
        b_base[slot] = b_base_in[slot]
        spread_place(s, slot)
        cotangent_rows[cell] = dot(order_in[slot], cotangent_ref[0, 0, cell]).astype(BF)
    for slot, rim in ((0, before_ref), (cells + 1, after_ref)):
        rim_place = rim[particles:, :].astype(F32)
        live[slot] = jnp.sum(rim_place[2:3, :]).astype(jnp.int32)
        order_slot(s, slot, rim[:particles, :], rim_place, None, None)
    aggregate[...] = aggregate_in[...]
    slope[...] = slope_in[...]
    slope_shift[...] = slope_shift_in[...]
    source_grad[...] = jnp.zeros_like(source_grad)
    shift[...] = jnp.zeros_like(shift)
    pair_of, set_bounds, over_range, weights_of, forward = pair_tools(s)
    set_bounds()
    forward(True)

    latent = s.rows[1 : cells + 1].reshape(count, width)
    agg_b = s.aggregate[...].reshape(count, width).astype(BF)
    message = dot(agg_b, edge_out_ref[...]).astype(BF)
    hidden_pre = (
        dot(latent, node_in_ref[:width, :])
        + dot(message, node_in_ref[width:, :])
        + node_in_bias_ref[...]
    )
    gate = sigmoid(hidden_pre)
    hidden_b = (hidden_pre * gate).astype(BF)
    pre_norm = dot(hidden_b, node_out_ref[...]) + node_out_bias_ref[...]
    centred = pre_norm - jnp.mean(pre_norm, axis=-1, keepdims=True)
    inverse = lax.rsqrt(jnp.mean(centred * centred, axis=-1, keepdims=True) + 1e-05)
    normed = centred * inverse
    gain = gain_ref[...]
    new_rows = (latent.astype(F32) + normed * gain).astype(BF)
    for cell in range(cells):
        there = new_rows[cell * particles : (cell + 1) * particles]
        new_latent_ref[0, 0, cell] = t_dot(s.order[cell + 1], there).astype(BF)

    cotangent = s.cotangent_rows[...].reshape(count, width).astype(F32)
    gain_sum = column_sum(cotangent * normed)
    scaled = cotangent * gain
    grad_pre = inverse * (
        scaled
        - jnp.mean(scaled, axis=-1, keepdims=True)
        - normed * jnp.mean(scaled * normed, axis=-1, keepdims=True)
    )
    grad_pre_b = grad_pre.astype(BF)
    out_bias_sum = column_sum(grad_pre)
    pack_ref[640:768, :] = t_dot(hidden_b, grad_pre_b).astype(BF)
    grad_hidden = dot_t(grad_pre_b, node_out_ref[...]) * (
        gate * (1.0 + hidden_pre * (1.0 - gate))
    )
    grad_hidden_b = grad_hidden.astype(BF)
    in_bias_sum = column_sum(grad_hidden)
    pack_ref[384:512, :] = t_dot(latent, grad_hidden_b).astype(BF)
    pack_ref[512:640, :] = t_dot(message, grad_hidden_b).astype(BF)
    grad_message = dot_t(grad_hidden_b, node_in_ref[width:, :]).astype(BF)
    pack_ref[256:384, :] = t_dot(agg_b, grad_message).astype(BF)
    upstream = dot_t(grad_message, edge_out_ref[...])
    s.upstream[...] = upstream.reshape(cells, particles, width)
    grad_rows = cotangent + dot_t(grad_hidden_b, node_in_ref[:width, :])
    s.aggregate[...] = grad_rows.reshape(cells, particles, width)

    def backward_pair(slot, _):
        target, source, off, alpha, beta = pair_of(slot)
        live_target = s.live[target + 1]
        live_source = s.live[source]
        shift_a = (0.5 * alpha) * offset_x
        shift_b = (0.5 * beta) * offset_x

        def block(index, _):
            first = pl.multiple_of(index * ROWS, ROWS)

            def visit(size, at):
                at = pl.multiple_of(at, STEP)
                a = (s.a_base[target, pl.ds(at, size), :] + shift_a).astype(BF)
                up = s.upstream[target, pl.ds(at, size), :].astype(BF)
                there = pltpu.roll(s.place[target + 1], particles - at, axis=1)

                def steep(row):
                    b = s.b_base[source, pl.ds(first + row, 1), :] + shift_b
                    u = jnp.broadcast_to(b.astype(BF), (size, width)) + a
                    t = jnp.tanh(u)
                    return up * (t + u * (1.0 - t * t))

                moved = jnp.zeros((GRAIN, width), F32)
                for group in range(0, ROWS, GRAIN):
                    here = pl.ds(first + group, GRAIN)
                    x, y = s.x[source, here, :], s.y[source, here, :]
                    weights = weights_of(
                        x, y, there, at, first + group, live_source, live_target, -off
                    )[:, :size]
                    total = jnp.zeros((GRAIN, width), F32)
                    for r in range(0, GRAIN, 2):
                        pair = jnp.concatenate([steep(group + r), steep(group + r + 1)], axis=1)
                        both = dot(weights, pair)
                        total = jnp.where(row_of == r, both[:, :width], total)
                        total = jnp.where(row_of == r + 1, both[:, width:], total)
                    total = 0.5 * (total + dot(weights, up))
                    s.source_grad[source, here, :] += total
                    moved = moved + total
                s.shift[...] += beta * (moved[:8] + moved[8:])

            over_range(slot, 2, first, live_source, visit)
            return 0

        lax.fori_loop(0, blocks(live_source, ROWS), block, 0)
        return 0

    lax.fori_loop(0, listed[0, 0], backward_pair, 0)

    upstream = s.upstream[...].reshape(count, width)
    target_grad = 0.5 * upstream * s.slope[...].reshape(count, width)
    target_b = target_grad.astype(BF)
    source_grad = s.source_grad[...].reshape(count + 2 * particles, width)
    source_b = source_grad.astype(BF)
    own_b = source_b[particles : particles + count]
    rim_grad_ref[0] = t_dot(s.order[0], source_b[:particles]).astype(BF)
    rim_grad_ref[1] = t_dot(s.order[cells + 1], source_b[particles + count :]).astype(BF)
    latent = s.rows[1 : cells + 1].reshape(count, width)
    pack_ref[0:128, :] = t_dot(latent, target_b).astype(BF)
    pack_ref[128:256, :] = (
        t_dot(latent, own_b)
        + t_dot(s.rows[0], source_b[:particles])
        + t_dot(s.rows[cells + 1], source_b[particles + count :])
    ).astype(BF)
    more = dot_t(target_b, s.target_w[...]) + dot_t(own_b, s.source_w[...])
    grad_rows = s.aggregate[...].reshape(count, width) + more
    for cell in range(cells):
        there = grad_rows[cell * particles : (cell + 1) * particles]
        coarse = there.astype(BF)
        fine = (there - coarse.astype(F32)).astype(BF)
        both = t_dot(s.order[cell + 1], jnp.concatenate([coarse, fine], axis=1))
        latent_grad_ref[0, 0, cell] = both[:, :width] + both[:, width:]
    x_target = s.x[1 : cells + 1].reshape(count, width)
    y_target = s.y[1 : cells + 1].reshape(count, width)
    x_source = s.x[...].reshape(count + 2 * particles, width)
    y_source = s.y[...].reshape(count + 2 * particles, width)
    shift = 0.5 * upstream * s.slope_shift[...].reshape(count, width)
    along = (
        column_sum(x_target * target_grad + shift)
        - column_sum(x_source * source_grad)
        + column_sum(s.shift[...])
    )
    across = column_sum((y_target - 0.5) * target_grad) - column_sum((y_source - 0.5) * source_grad)
    small = jnp.concatenate(
        [
            along,
            across,
            column_sum(target_grad),
            in_bias_sum,
            out_bias_sum,
            gain_sum,
            jnp.zeros((2, width), F32),
        ],
        axis=0,
    )
    coarse = small.astype(BF).astype(F32)
    pack_ref[768:784, :] = jnp.concatenate([coarse, small - coarse], axis=0).astype(BF)
    pack_ref[784:800, :] = jnp.zeros((16, width), BF)


def whole(array):
    return pl.BlockSpec(array.shape, lambda step: (0,) * len(array.shape))


def run_own(scalars, arrays, cells, particles, width):
    smem = pl.BlockSpec(memory_space=pltpu.SMEM)
    vmem = pl.BlockSpec(memory_space=pltpu.VMEM)
    window = cells + 2
    tile = (particles, width)
    pairs = scalars[1].shape[-1]
    outs = [
        jax.ShapeDtypeStruct((window, META, particles), F32),
        jax.ShapeDtypeStruct((window,) + tile, BF),
        jax.ShapeDtypeStruct((window,) + tile, BF),
        jax.ShapeDtypeStruct((cells,) + tile, F32),
        jax.ShapeDtypeStruct((window,) + tile, F32),
        jax.ShapeDtypeStruct((cells,) + tile, F32),
        jax.ShapeDtypeStruct((cells,) + tile, F32),
        jax.ShapeDtypeStruct((cells,) + tile, F32),
    ]
    return pl.pallas_call(
        own_kernel,
        grid=(1,),
        in_specs=[smem] * len(scalars)
        + [vmem if place == 1 else whole(array) for place, array in enumerate(arrays)],
        out_specs=[vmem] * len(outs),
        out_shape=outs,
        scratch_shapes=[
            pltpu.SMEM((window,), jnp.int32),
            pltpu.VMEM((window,) + tile, F32),
            pltpu.VMEM((window,) + tile, F32),
            pltpu.VMEM((pairs, 8, particles), jnp.int32),
            pltpu.SMEM((pairs, 8, particles), jnp.int32),
            pltpu.SemaphoreType.DMA,
        ],
        compiler_params=pltpu.CompilerParams(vmem_limit_bytes=24 << 20),
        cost_estimate=pl.CostEstimate(
            flops=1 << 31, bytes_accessed=1 << 21, transcendentals=1 << 24
        ),
        name="own",
    )(*scalars, *arrays)


def run_step(scalars, arrays, latent, cells, particles, width):
    smem = pl.BlockSpec(memory_space=pltpu.SMEM)
    vmem = pl.BlockSpec(memory_space=pltpu.VMEM)
    window = cells + 2
    tile = (particles, width)
    pairs = scalars[1].shape[-1]
    resident = (0, 1) + tuple(range(3, 11))
    outs = [
        jax.ShapeDtypeStruct(latent.shape, BF),
        jax.ShapeDtypeStruct(latent.shape, F32),
        jax.ShapeDtypeStruct((2,) + tile, BF),
        jax.ShapeDtypeStruct((PACK_ROWS, width), BF),
    ]
    return pl.pallas_call(
        step_kernel,
        grid=(1,),
        in_specs=[smem] * len(scalars)
        + [vmem if place in resident else whole(array) for place, array in enumerate(arrays)],
        out_specs=[whole(array) for array in outs[:2]] + [vmem, vmem],
        out_shape=outs,
        scratch_shapes=[
            pltpu.SMEM((window,), jnp.int32),
            pltpu.VMEM((window, META, particles), F32),
            pltpu.VMEM((window,) + tile, BF),
            pltpu.VMEM((window,) + tile, BF),
            pltpu.VMEM((window,) + tile, F32),
            pltpu.VMEM((cells,) + tile, F32),
            pltpu.VMEM((cells,) + tile, F32),
            pltpu.VMEM((cells,) + tile, F32),
            pltpu.VMEM((window,) + tile, F32),
            pltpu.VMEM((window,) + tile, F32),
            pltpu.VMEM((cells,) + tile, F32),
            pltpu.VMEM((window,) + tile, F32),
            pltpu.VMEM((8, width), F32),
            pltpu.VMEM((cells,) + tile, BF),
            pltpu.VMEM((pairs, 8, particles), jnp.int32),
            pltpu.SMEM((pairs, 8, particles), jnp.int32),
            pltpu.SemaphoreType.DMA,
        ],
        compiler_params=pltpu.CompilerParams(vmem_limit_bytes=24 << 20),
        name="step",
    )(*scalars, *arrays)


def finish_kernel(
    core_ref,
    mine_ref,
    other_ref,
    partial_ref,
    rims_ref,
    source_w_ref,
    latent_grad_ref,
    target_w_out,
    source_w_out,
    offset_out,
    bias_out,
    edge_out_out,
    node_in_out,
    in_bias_out,
    node_out_out,
    out_bias_out,
    gain_out,
    *,
    scale,
):
    cells = partial_ref.shape[2]
    mine = mine_ref[...].astype(F32)
    other = other_ref[...].astype(F32)
    first = core_ref[0] == 0
    low = jnp.where(first, mine, other) * scale
    high = jnp.where(first, other, mine) * scale
    whole = jnp.concatenate([low, high], axis=0)
    target_w_out[...] = whole[0:128]
    source_w_out[...] = whole[128:256]
    edge_out_out[...] = whole[256:384]
    node_in_out[...] = whole[384:640]
    node_out_out[...] = whole[640:768]
    small = whole[768:776] + whole[776:784]
    offset_out[...] = small[0:2]
    bias_out[...] = small[2:3]
    in_bias_out[...] = small[3:4]
    out_bias_out[...] = small[4:5]
    gain_out[...] = small[5:6]
    latent_grad_ref[...] = partial_ref[...]
    latent_grad_ref[0, 0, cells - 1] += dot_t(rims_ref[0], source_w_ref[...])
    latent_grad_ref[0, 0, 0] += dot_t(rims_ref[1], source_w_ref[...])


def run_finish(core, mine, other, partial, rims, source_w, scale):
    width = mine.shape[-1]
    vmem = pl.BlockSpec(memory_space=pltpu.VMEM)
    smem = pl.BlockSpec(memory_space=pltpu.SMEM)
    square = jax.ShapeDtypeStruct((width, width), F32)
    row = jax.ShapeDtypeStruct((1, width), F32)
    return pl.pallas_call(
        functools.partial(finish_kernel, scale=scale),
        in_specs=[smem] + [vmem] * 5,
        out_specs=[vmem] * 11,
        out_shape=[
            jax.ShapeDtypeStruct(partial.shape, F32),
            square,
            square,
            jax.ShapeDtypeStruct((2, width), F32),
            row,
            square,
            jax.ShapeDtypeStruct((2 * width, width), F32),
            row,
            square,
            row,
            row,
        ],
        compiler_params=pltpu.CompilerParams(vmem_limit_bytes=32 << 20),
        name="finish",
    )(core, mine, other, partial, rims, source_w)


def neighbours(axis, by):
    length = lax.axis_size(axis)
    return [(i, i + by) for i in range(length) if 0 <= i + by < length]


def swap_cores(array):
    size = lax.axis_size("wide")
    return lax.ppermute(array, "wide", [(i, i ^ 1) for i in range(size)])


def exchange(array, axis, groups=None):
    return lax.all_to_all(array, axis, 0, 0, axis_index_groups=groups, tiled=True)


def spread(array, count):
    return jnp.broadcast_to(array[None], (count,) + array.shape)


def sum_everywhere(pack, core, first):
    width = pack.shape[-1]
    space = lax.axis_size("space")
    wide = lax.axis_size("wide")
    fellows = [list(range(start, wide, 2)) for start in range(2)]
    halves = pack.reshape(2, -1, width)
    mine = jnp.where(core == 0, halves[0], halves[1])
    sent = jnp.where(core == 0, halves[1], halves[0])
    half = mine.astype(F32) + swap_cores(sent).astype(F32)
    parts = half.astype(BF).reshape(space, -1, width)
    parts, *first = lax.optimization_barrier((parts,) + first)
    part = jnp.sum(exchange(parts, "space").astype(F32), axis=0).astype(BF)
    others = exchange(spread(part, wide // 2), "wide", fellows)
    part = jnp.sum(others.astype(F32), axis=0).astype(BF)
    return exchange(spread(part, space), "space").reshape(-1, width), *first


def on_device(
    latent,
    coords,
    cell_counts,
    pair_target,
    pair_source,
    pair_count,
    edge_target_w,
    edge_source_w,
    edge_offset,
    edge_bias,
    edge_out,
    node_in,
    node_in_bias,
    node_out,
    node_out_bias,
    norm_gain,
    cotangent,
):
    cells, particles, width = latent.shape[2:]
    core = lax.rem(lax.axis_index("wide"), 2)
    live = (
        jnp.arange(particles, dtype=jnp.int32)[None, :] < cell_counts[0, 0][:, None]
    ).astype(BF)
    meta = jnp.concatenate(
        [coords[0, 0], live[:, None, :], jnp.zeros((cells, META - 3, particles), BF)], axis=1
    )
    last = jnp.concatenate([latent[0, 0, cells - 1], meta[cells - 1]], axis=0)
    initial = jnp.concatenate([latent[0, 0, 0], meta[0]], axis=0)
    before = lax.ppermute(last, "space", neighbours("space", 1))
    after = lax.ppermute(initial, "space", neighbours("space", -1))
    scalars = (cell_counts, pair_target, pair_source, pair_count)
    state = run_own(
        scalars,
        (latent, meta, edge_target_w, edge_source_w, edge_offset, edge_bias[None, :]),
        cells,
        particles,
        width,
    )
    new_rows, partial, rims, pack = run_step(
        scalars,
        (before, after, cotangent)
        + tuple(state)
        + (
            edge_target_w,
            edge_source_w,
            edge_offset,
            edge_out,
            node_in,
            node_in_bias[None, :],
            node_out,
            node_out_bias[None, :],
            norm_gain[None, :],
        ),
        latent,
        cells,
        particles,
        width,
    )
    from_next = lax.ppermute(rims[0], "space", neighbours("space", -1))
    from_prev = lax.ppermute(rims[1], "space", neighbours("space", 1))
    mine, from_next, from_prev = sum_everywhere(pack, core, (from_next, from_prev))
    other = swap_cores(mine)
    scale = 1.0 / math.sqrt(lax.axis_size("space") * lax.axis_size("wide") * cells * particles)
    rims_in = jnp.stack([from_next, from_prev])
    outs = run_finish(
        core.astype(jnp.int32)[None], mine, other, partial, rims_in, edge_source_w, scale
    )
    (latent_grad, target_w, source_w, offset, bias, out_w, in_w, in_bias, node_w, out_bias, gain) = outs
    return (
        new_rows,
        latent_grad,
        target_w,
        source_w,
        offset,
        bias[0],
        out_w,
        in_w,
        in_bias[0],
        node_w,
        out_bias[0],
        gain[0],
    )


def solution(mesh):
    cell = P("wide", "space", None, None, None)
    table = P("wide", "space", None)
    return jax.shard_map(
        on_device,
        mesh=mesh,
        in_specs=(cell, cell, table, table, table, P("wide", "space")) + (P(),) * 10 + (cell,),
        out_specs=(cell, cell) + (P(),) * 10,
        check_vma=False,
    )
```

```python
import functools
import math
import types

import jax
import jax.numpy as jnp
from jax import lax
from jax.experimental import pallas as pl
from jax.experimental.pallas import tpu as pltpu
from jax.sharding import PartitionSpec as P

BF = jnp.bfloat16
F32 = jnp.float32
META = 16
GRAIN = 16
STEP = 16
ROWS = 64
PACK_ROWS = 800


def dot(a, b):
    return jnp.dot(a, b, preferred_element_type=F32)


def dot_t(a, b):
    return lax.dot_general(a, b, (((1,), (1,)), ((), ())), preferred_element_type=F32)


def t_dot(a, b):
    return lax.dot_general(a, b, (((0,), (0,)), ((), ())), preferred_element_type=F32)


def sigmoid(v):
    return 0.5 * (1.0 + jnp.tanh(0.5 * v))


def blocks(count, rows):
    return lax.div(count + (rows - 1), rows)


def column_sum(values):
    return jnp.sum(values, axis=0, keepdims=True)


def order_slot(s, slot, rows_in, place, target_w, bias):
    particles = place.shape[1]
    width = rows_in.shape[1]
    sub = lax.broadcasted_iota(jnp.int32, (particles, particles), 0)
    lane = lax.broadcasted_iota(jnp.int32, (particles, particles), 1)
    pick = lax.broadcasted_iota(jnp.int32, (META, width), 0)
    pick_key = jnp.where(pick == 3, 1.0, 0.0).astype(BF)
    key = jnp.where(place[2:3, :] > 0.5, place[0:1, :], 2.0)
    place = jnp.where(pick == 3, key, place).astype(BF)
    keys = t_dot(place, pick_key)
    ahead = (keys < key) | ((keys == key) & (sub < lane))
    rank = column_sum(jnp.where(ahead, 1.0, 0.0))
    order = jnp.where(sub.astype(F32) == rank, 1.0, 0.0).astype(BF)
    s.order[slot] = order
    s.place[slot] = dot_t(place, order)
    spread_place(s, slot)
    moved = s.x[slot] * s.offset[0:1, :] + (s.y[slot] - 0.5) * s.offset[1:2, :]
    rows_in = dot(order, rows_in).astype(BF)
    s.rows[slot] = rows_in
    proj_source = dot(rows_in, s.source_w[...]).astype(BF).astype(F32)
    s.b_base[slot] = 0.5 * (proj_source - moved)
    if target_w is not None:
        proj_target = (dot(rows_in, target_w[...]) + bias[...]).astype(BF)
        s.a_base[slot - 1] = 0.5 * (proj_target.astype(F32) + moved)


def spread_place(s, slot):
    pick = lax.broadcasted_iota(jnp.int32, s.place.shape[1:], 0)
    place = s.place[slot].astype(BF)
    s.x[slot] = t_dot(place, jnp.where(pick == 0, 1.0, 0.0).astype(BF))
    s.y[slot] = t_dot(place, jnp.where(pick == 1, 1.0, 0.0).astype(BF))


def pair_tools(s):
    particles, width = s.x.shape[1:]
    cells = s.a_base.shape[0]
    offset_x = s.offset[0:1, :]
    row_of = lax.broadcasted_iota(jnp.int32, (GRAIN, width), 0)
    sub = lax.broadcasted_iota(jnp.int32, (particles, particles), 0)
    listed = s.listed[0, 0]

    def pair_of(slot):
        target = s.targets[0, 0, slot]
        source = s.sources[0, 0, slot]
        off = (target - source + 1).astype(F32)
        alpha = jnp.where(off < -0.5, -1.0, jnp.where(off > 0.5, 0.0, -0.5))
        return target, source, off, alpha, off - alpha

    def bound_pair(slot, _):
        target, source, off, _, _ = pair_of(slot)
        live_target = s.live[target + 1]
        live_source = s.live[source]

        def counted(hit):
            return column_sum(jnp.where(hit, 1.0, 0.0)).astype(jnp.int32)

        x_target, row_target = s.x[target + 1], s.place[target + 1, 0:1, :]
        x_source, row_source = s.x[source], s.place[source, 0:1, :]
        zero = jnp.zeros((1, particles), jnp.int32)
        source_at_most = counted((x_source <= row_target) & (sub < live_source))
        source_below = counted((x_source < row_target) & (sub < live_source))
        target_at_most = counted((x_target <= row_source) & (sub < live_target))
        target_below = counted((x_target < row_source) & (sub < live_target))
        s.bounds[slot] = jnp.concatenate(
            [
                jnp.where(off > 0.5, source_at_most, zero),
                jnp.where(off < -0.5, source_below, zero + live_source),
                jnp.where(off < -0.5, target_at_most, zero),
                jnp.where(off > 0.5, target_below, zero + live_target),
                jnp.zeros((4, particles), jnp.int32),
            ],
            axis=0,
        )
        return 0

    def over_pairs(rim, pair):
        def visit(slot, _):
            source = s.sources[0, 0, slot]
            at_rim = (source == 0) | (source == cells + 1)

            @pl.when(at_rim == rim)
            def _():
                pair(slot, 0)

            return 0

        lax.fori_loop(0, listed, visit, 0)

    def set_bounds(rim):
        over_pairs(rim, bound_pair)
        copy = pltpu.make_async_copy(s.bounds, s.bounds_smem, s.bounds_sem)
        copy.start()
        copy.wait()

    def over_range(slot, which, first, live, visit):
        last = jnp.minimum(first + (ROWS - 1), live - 1)
        start = lax.div(s.bounds_smem[slot, which, first], STEP)
        most = particles // STEP
        size = jnp.clip(blocks(s.bounds_smem[slot, which + 1, last], STEP) - start, 0, most)
        lax.switch(
            size,
            [lambda at: None]
            + [functools.partial(visit, STEP * count) for count in range(1, most + 1)],
            jnp.clip(start, 0, most - size) * STEP,
        )

    lane_rows = lax.broadcasted_iota(jnp.int32, (GRAIN, particles), 1)

    def weights_of(x, y, there, at, first, live_here, live_there, shift):
        dx = (shift + x) - there[0:1, :]
        dy = y - there[1:2, :]
        near = jnp.maximum(1.0 - dx * dx - dy * dy, 0.0)
        keep = (row_of + first < live_here) & (lane_rows + at < live_there)
        return jnp.where(keep, near * near, 0.0).astype(BF)

    def forward_pair(slot, _):
        target, source, off, alpha, beta = pair_of(slot)
        live_target = s.live[target + 1]
        live_source = s.live[source]
        shift_a = (0.5 * alpha) * offset_x
        shift_b = (0.5 * beta) * offset_x

        def block(index, _):
            first = pl.multiple_of(index * ROWS, ROWS)

            def visit(size, at):
                at = pl.multiple_of(at, STEP)
                b = (s.b_base[source, pl.ds(at, size), :] + shift_b).astype(BF)
                there = pltpu.roll(s.place[source], particles - at, axis=1)
                for group in range(0, ROWS, GRAIN):
                    here = pl.ds(first + group, GRAIN)
                    x, y = s.x[target + 1, here, :], s.y[target + 1, here, :]
                    weights = weights_of(
                        x, y, there, at, first + group, live_target, live_source, off
                    )
                    total = jnp.zeros((GRAIN, 2 * width), F32)
                    for r in range(GRAIN):
                        a = s.a_base[target, pl.ds(first + group + r, 1), :] + shift_a
                        u = jnp.broadcast_to(a.astype(BF), (size, width)) + b
                        t = jnp.tanh(u)
                        bent = u + u * t
                        steep = 1.0 + (t + u * (1.0 - t * t))
                        one = jnp.where(row_of == r, weights, jnp.zeros_like(weights))
                        total = total + dot(
                            one[:, :size], jnp.concatenate([bent, steep], axis=1)
                        )
                    s.aggregate[target, here, :] += total[:, :width]
                    s.slope[target, here, :] += total[:, width:]
                    s.slope_shift[target, here, :] += alpha * total[:, width:]

            over_range(slot, 0, first, live_target, visit)
            return 0

        lax.fori_loop(0, blocks(live_target, ROWS), block, 0)
        return 0

    def forward(rim):
        over_pairs(rim, forward_pair)

    return pair_of, set_bounds, over_range, weights_of, forward


def own_kernel(
    counts,
    targets,
    sources,
    listed,
    latent_ref,
    meta_ref,
    target_w,
    source_w,
    offset,
    bias,
    place,
    order,
    rows,
    a_base,
    b_base,
    aggregate,
    slope,
    slope_shift,
    bounds,
    live,
    x,
    y,
    bounds_smem,
    bounds_sem,
):
    s = types.SimpleNamespace(**locals())
    cells = latent_ref.shape[2]
    live[0] = 0
    live[cells + 1] = 0
    for cell in range(cells):
        live[cell + 1] = counts[0, 0, cell]
        order_slot(
            s, cell + 1, latent_ref[0, 0, cell], meta_ref[cell].astype(F32), target_w, bias
        )
    for slot in (0, cells + 1):
        place[slot] = jnp.zeros(place.shape[1:], F32)
        order[slot] = jnp.zeros(order.shape[1:], BF)
        rows[slot] = jnp.zeros(rows.shape[1:], BF)
        b_base[slot] = jnp.zeros(b_base.shape[1:], F32)
        x[slot] = jnp.zeros(x.shape[1:], F32)
        y[slot] = jnp.zeros(y.shape[1:], F32)
    aggregate[...] = jnp.zeros_like(aggregate)
    slope[...] = jnp.zeros_like(slope)
    slope_shift[...] = jnp.zeros_like(slope_shift)
    _, set_bounds, _, _, forward = pair_tools(s)
    bounds[...] = jnp.zeros_like(bounds)
    set_bounds(False)
    forward(False)


def step_kernel(
    counts,
    targets,
    sources,
    listed,
    before_ref,
    after_ref,
    cotangent_ref,
    place_in,
    order_in,
    rows_in,
    a_base,
    b_base_in,
    aggregate_in,
    slope_in,
    slope_shift_in,
    bounds_in,
    target_w,
    source_w,
    offset,
    edge_out_ref,
    node_in_ref,
    node_in_bias_ref,
    node_out_ref,
    node_out_bias_ref,
    gain_ref,
    new_latent_ref,
    latent_grad_ref,
    rim_grad_ref,
    pack_ref,
    live,
    place,
    order,
    rows,
    b_base,
    aggregate,
    slope,
    slope_shift,
    x,
    y,
    upstream_all,
    source_grad,
    shift,
    cotangent_rows,
    bounds,
    bounds_smem,
    bounds_sem,
):
    s = types.SimpleNamespace(**locals())
    s.upstream = upstream_all
    cells, particles, width = cotangent_ref.shape[2:]
    count = cells * particles
    row_of = lax.broadcasted_iota(jnp.int32, (GRAIN, width), 0)
    offset_x = offset[0:1, :]
    for cell in range(cells):
        slot = cell + 1
        live[slot] = counts[0, 0, cell]
        place[slot] = place_in[slot]
        order[slot] = order_in[slot]
        rows[slot] = rows_in[slot]
        b_base[slot] = b_base_in[slot]
        spread_place(s, slot)
        cotangent_rows[cell] = dot(order_in[slot], cotangent_ref[0, 0, cell]).astype(BF)
    for slot, rim in ((0, before_ref), (cells + 1, after_ref)):
        rim_place = rim[particles:, :].astype(F32)
        live[slot] = jnp.sum(rim_place[2:3, :]).astype(jnp.int32)
        order_slot(s, slot, rim[:particles, :], rim_place, None, None)
    aggregate[...] = aggregate_in[...]
    slope[...] = slope_in[...]
    slope_shift[...] = slope_shift_in[...]
    source_grad[...] = jnp.zeros_like(source_grad)
    shift[...] = jnp.zeros_like(shift)
    pair_of, set_bounds, over_range, weights_of, forward = pair_tools(s)
    bounds[...] = bounds_in[...]
    set_bounds(True)
    forward(True)

    latent = s.rows[1 : cells + 1].reshape(count, width)
    agg_b = s.aggregate[...].reshape(count, width).astype(BF)
    message = dot(agg_b, edge_out_ref[...]).astype(BF)
    hidden_pre = (
        dot(latent, node_in_ref[:width, :])
        + dot(message, node_in_ref[width:, :])
        + node_in_bias_ref[...]
    )
    gate = sigmoid(hidden_pre)
    hidden_b = (hidden_pre * gate).astype(BF)
    pre_norm = dot(hidden_b, node_out_ref[...]) + node_out_bias_ref[...]
    centred = pre_norm - jnp.mean(pre_norm, axis=-1, keepdims=True)
    inverse = lax.rsqrt(jnp.mean(centred * centred, axis=-1, keepdims=True) + 1e-05)
    normed = centred * inverse
    gain = gain_ref[...]
    new_rows = (latent.astype(F32) + normed * gain).astype(BF)
    for cell in range(cells):
        there = new_rows[cell * particles : (cell + 1) * particles]
        new_latent_ref[0, 0, cell] = t_dot(s.order[cell + 1], there).astype(BF)

    cotangent = s.cotangent_rows[...].reshape(count, width).astype(F32)
    gain_sum = column_sum(cotangent * normed)
    scaled = cotangent * gain
    grad_pre = inverse * (
        scaled
        - jnp.mean(scaled, axis=-1, keepdims=True)
        - normed * jnp.mean(scaled * normed, axis=-1, keepdims=True)
    )
    grad_pre_b = grad_pre.astype(BF)
    out_bias_sum = column_sum(grad_pre)
    pack_ref[640:768, :] = t_dot(hidden_b, grad_pre_b).astype(BF)
    grad_hidden = dot_t(grad_pre_b, node_out_ref[...]) * (
        gate * (1.0 + hidden_pre * (1.0 - gate))
    )
    grad_hidden_b = grad_hidden.astype(BF)
    in_bias_sum = column_sum(grad_hidden)
    pack_ref[384:512, :] = t_dot(latent, grad_hidden_b).astype(BF)
    pack_ref[512:640, :] = t_dot(message, grad_hidden_b).astype(BF)
    grad_message = dot_t(grad_hidden_b, node_in_ref[width:, :]).astype(BF)
    pack_ref[256:384, :] = t_dot(agg_b, grad_message).astype(BF)
    upstream = dot_t(grad_message, edge_out_ref[...])
    s.upstream[...] = upstream.reshape(cells, particles, width)
    grad_rows = cotangent + dot_t(grad_hidden_b, node_in_ref[:width, :])
    s.aggregate[...] = grad_rows.reshape(cells, particles, width)

    def backward_pair(slot, _):
        target, source, off, alpha, beta = pair_of(slot)
        live_target = s.live[target + 1]
        live_source = s.live[source]
        shift_a = (0.5 * alpha) * offset_x
        shift_b = (0.5 * beta) * offset_x

        def block(index, _):
            first = pl.multiple_of(index * ROWS, ROWS)

            def visit(size, at):
                at = pl.multiple_of(at, STEP)
                a = (s.a_base[target, pl.ds(at, size), :] + shift_a).astype(BF)
                up = s.upstream[target, pl.ds(at, size), :].astype(BF)
                there = pltpu.roll(s.place[target + 1], particles - at, axis=1)

                def steep(row):
                    b = s.b_base[source, pl.ds(first + row, 1), :] + shift_b
                    u = jnp.broadcast_to(b.astype(BF), (size, width)) + a
                    t = jnp.tanh(u)
                    return up * (t + u * (1.0 - t * t))

                moved = jnp.zeros((GRAIN, width), F32)
                for group in range(0, ROWS, GRAIN):
                    here = pl.ds(first + group, GRAIN)
                    x, y = s.x[source, here, :], s.y[source, here, :]
                    weights = weights_of(
                        x, y, there, at, first + group, live_source, live_target, -off
                    )[:, :size]
                    total = jnp.zeros((GRAIN, width), F32)
                    for r in range(0, GRAIN, 2):
                        pair = jnp.concatenate([steep(group + r), steep(group + r + 1)], axis=1)
                        both = dot(weights, pair)
                        total = jnp.where(row_of == r, both[:, :width], total)
                        total = jnp.where(row_of == r + 1, both[:, width:], total)
                    total = 0.5 * (total + dot(weights, up))
                    s.source_grad[source, here, :] += total
                    moved = moved + total
                s.shift[...] += beta * (moved[:8] + moved[8:])

            over_range(slot, 2, first, live_source, visit)
            return 0

        lax.fori_loop(0, blocks(live_source, ROWS), block, 0)
        return 0

    lax.fori_loop(0, listed[0, 0], backward_pair, 0)

    upstream = s.upstream[...].reshape(count, width)
    target_grad = 0.5 * upstream * s.slope[...].reshape(count, width)
    target_b = target_grad.astype(BF)
    source_grad = s.source_grad[...].reshape(count + 2 * particles, width)
    source_b = source_grad.astype(BF)
    own_b = source_b[particles : particles + count]
    rim_grad_ref[0] = t_dot(s.order[0], source_b[:particles]).astype(BF)
    rim_grad_ref[1] = t_dot(s.order[cells + 1], source_b[particles + count :]).astype(BF)
    latent = s.rows[1 : cells + 1].reshape(count, width)
    pack_ref[0:128, :] = t_dot(latent, target_b).astype(BF)
    pack_ref[128:256, :] = (
        t_dot(latent, own_b)
        + t_dot(s.rows[0], source_b[:particles])
        + t_dot(s.rows[cells + 1], source_b[particles + count :])
    ).astype(BF)
    more = dot_t(target_b, s.target_w[...]) + dot_t(own_b, s.source_w[...])
    grad_rows = s.aggregate[...].reshape(count, width) + more
    for cell in range(cells):
        there = grad_rows[cell * particles : (cell + 1) * particles]
        coarse = there.astype(BF)
        fine = (there - coarse.astype(F32)).astype(BF)
        both = t_dot(s.order[cell + 1], jnp.concatenate([coarse, fine], axis=1))
        latent_grad_ref[0, 0, cell] = both[:, :width] + both[:, width:]
    x_target = s.x[1 : cells + 1].reshape(count, width)
    y_target = s.y[1 : cells + 1].reshape(count, width)
    x_source = s.x[...].reshape(count + 2 * particles, width)
    y_source = s.y[...].reshape(count + 2 * particles, width)
    shift = 0.5 * upstream * s.slope_shift[...].reshape(count, width)
    along = (
        column_sum(x_target * target_grad + shift)
        - column_sum(x_source * source_grad)
        + column_sum(s.shift[...])
    )
    across = column_sum((y_target - 0.5) * target_grad) - column_sum((y_source - 0.5) * source_grad)
    small = jnp.concatenate(
        [
            along,
            across,
            column_sum(target_grad),
            in_bias_sum,
            out_bias_sum,
            gain_sum,
            jnp.zeros((2, width), F32),
        ],
        axis=0,
    )
    coarse = small.astype(BF).astype(F32)
    pack_ref[768:784, :] = jnp.concatenate([coarse, small - coarse], axis=0).astype(BF)
    pack_ref[784:800, :] = jnp.zeros((16, width), BF)


def whole(array):
    return pl.BlockSpec(array.shape, lambda step: (0,) * len(array.shape))


def run_own(scalars, arrays, cells, particles, width):
    smem = pl.BlockSpec(memory_space=pltpu.SMEM)
    vmem = pl.BlockSpec(memory_space=pltpu.VMEM)
    window = cells + 2
    tile = (particles, width)
    pairs = scalars[1].shape[-1]
    outs = [
        jax.ShapeDtypeStruct((window, META, particles), F32),
        jax.ShapeDtypeStruct((window,) + tile, BF),
        jax.ShapeDtypeStruct((window,) + tile, BF),
        jax.ShapeDtypeStruct((cells,) + tile, F32),
        jax.ShapeDtypeStruct((window,) + tile, F32),
        jax.ShapeDtypeStruct((cells,) + tile, F32),
        jax.ShapeDtypeStruct((cells,) + tile, F32),
        jax.ShapeDtypeStruct((cells,) + tile, F32),
        jax.ShapeDtypeStruct((pairs, 8, particles), jnp.int32),
    ]
    return pl.pallas_call(
        own_kernel,
        grid=(1,),
        in_specs=[smem] * len(scalars)
        + [vmem if place == 1 else whole(array) for place, array in enumerate(arrays)],
        out_specs=[vmem] * len(outs),
        out_shape=outs,
        scratch_shapes=[
            pltpu.SMEM((window,), jnp.int32),
            pltpu.VMEM((window,) + tile, F32),
            pltpu.VMEM((window,) + tile, F32),
            pltpu.SMEM((pairs, 8, particles), jnp.int32),
            pltpu.SemaphoreType.DMA,
        ],
        compiler_params=pltpu.CompilerParams(vmem_limit_bytes=24 << 20),
        cost_estimate=pl.CostEstimate(
            flops=1 << 31, bytes_accessed=1 << 21, transcendentals=1 << 24
        ),
        name="own",
    )(*scalars, *arrays)


def run_step(scalars, arrays, latent, cells, particles, width):
    smem = pl.BlockSpec(memory_space=pltpu.SMEM)
    vmem = pl.BlockSpec(memory_space=pltpu.VMEM)
    window = cells + 2
    tile = (particles, width)
    pairs = scalars[1].shape[-1]
    resident = (0, 1) + tuple(range(3, 12))
    outs = [
        jax.ShapeDtypeStruct(latent.shape, BF),
        jax.ShapeDtypeStruct(latent.shape, F32),
        jax.ShapeDtypeStruct((2,) + tile, BF),
        jax.ShapeDtypeStruct((PACK_ROWS, width), BF),
    ]
    return pl.pallas_call(
        step_kernel,
        grid=(1,),
        in_specs=[smem] * len(scalars)
        + [vmem if place in resident else whole(array) for place, array in enumerate(arrays)],
        out_specs=[whole(array) for array in outs[:2]] + [vmem, vmem],
        out_shape=outs,
        scratch_shapes=[
            pltpu.SMEM((window,), jnp.int32),
            pltpu.VMEM((window, META, particles), F32),
            pltpu.VMEM((window,) + tile, BF),
            pltpu.VMEM((window,) + tile, BF),
            pltpu.VMEM((window,) + tile, F32),
            pltpu.VMEM((cells,) + tile, F32),
            pltpu.VMEM((cells,) + tile, F32),
            pltpu.VMEM((cells,) + tile, F32),
            pltpu.VMEM((window,) + tile, F32),
            pltpu.VMEM((window,) + tile, F32),
            pltpu.VMEM((cells,) + tile, F32),
            pltpu.VMEM((window,) + tile, F32),
            pltpu.VMEM((8, width), F32),
            pltpu.VMEM((cells,) + tile, BF),
            pltpu.VMEM((pairs, 8, particles), jnp.int32),
            pltpu.SMEM((pairs, 8, particles), jnp.int32),
            pltpu.SemaphoreType.DMA,
        ],
        compiler_params=pltpu.CompilerParams(vmem_limit_bytes=24 << 20),
        name="step",
    )(*scalars, *arrays)


def finish_kernel(
    core_ref,
    mine_ref,
    other_ref,
    partial_ref,
    rims_ref,
    source_w_ref,
    latent_grad_ref,
    target_w_out,
    source_w_out,
    offset_out,
    bias_out,
    edge_out_out,
    node_in_out,
    in_bias_out,
    node_out_out,
    out_bias_out,
    gain_out,
    *,
    scale,
):
    cells = partial_ref.shape[2]
    mine = mine_ref[...].astype(F32)
    other = other_ref[...].astype(F32)
    first = core_ref[0] == 0
    low = jnp.where(first, mine, other) * scale
    high = jnp.where(first, other, mine) * scale
    whole = jnp.concatenate([low, high], axis=0)
    target_w_out[...] = whole[0:128]
    source_w_out[...] = whole[128:256]
    edge_out_out[...] = whole[256:384]
    node_in_out[...] = whole[384:640]
    node_out_out[...] = whole[640:768]
    small = whole[768:776] + whole[776:784]
    offset_out[...] = small[0:2]
    bias_out[...] = small[2:3]
    in_bias_out[...] = small[3:4]
    out_bias_out[...] = small[4:5]
    gain_out[...] = small[5:6]
    latent_grad_ref[...] = partial_ref[...]
    latent_grad_ref[0, 0, cells - 1] += dot_t(rims_ref[0], source_w_ref[...])
    latent_grad_ref[0, 0, 0] += dot_t(rims_ref[1], source_w_ref[...])


def run_finish(core, mine, other, partial, rims, source_w, scale):
    width = mine.shape[-1]
    vmem = pl.BlockSpec(memory_space=pltpu.VMEM)
    smem = pl.BlockSpec(memory_space=pltpu.SMEM)
    square = jax.ShapeDtypeStruct((width, width), F32)
    row = jax.ShapeDtypeStruct((1, width), F32)
    return pl.pallas_call(
        functools.partial(finish_kernel, scale=scale),
        in_specs=[smem] + [vmem] * 5,
        out_specs=[vmem] * 11,
        out_shape=[
            jax.ShapeDtypeStruct(partial.shape, F32),
            square,
            square,
            jax.ShapeDtypeStruct((2, width), F32),
            row,
            square,
            jax.ShapeDtypeStruct((2 * width, width), F32),
            row,
            square,
            row,
            row,
        ],
        compiler_params=pltpu.CompilerParams(vmem_limit_bytes=32 << 20),
        name="finish",
    )(core, mine, other, partial, rims, source_w)


def neighbours(axis, by):
    length = lax.axis_size(axis)
    return [(i, i + by) for i in range(length) if 0 <= i + by < length]


def swap_cores(array):
    size = lax.axis_size("wide")
    return lax.ppermute(array, "wide", [(i, i ^ 1) for i in range(size)])


def exchange(array, axis, groups=None):
    return lax.all_to_all(array, axis, 0, 0, axis_index_groups=groups, tiled=True)


def spread(array, count):
    return jnp.broadcast_to(array[None], (count,) + array.shape)


def sum_everywhere(pack, core, first):
    width = pack.shape[-1]
    space = lax.axis_size("space")
    wide = lax.axis_size("wide")
    columns = [list(range(start, wide, 4)) for start in range(4)]
    across = [(i, i ^ 2) for i in range(wide)]
    halves = pack.reshape(2, -1, width)
    mine = jnp.where(core == 0, halves[0], halves[1])
    sent = jnp.where(core == 0, halves[1], halves[0])
    half = mine.astype(F32) + swap_cores(sent).astype(F32)
    parts = half.astype(BF).reshape(space, -1, width)
    parts, *first = lax.optimization_barrier((parts,) + first)
    part = jnp.sum(exchange(parts, "space").astype(F32), axis=0).astype(BF)
    part = (part.astype(F32) + lax.ppermute(part, "wide", across).astype(F32)).astype(BF)
    others = exchange(spread(part, wide // 4), "wide", columns)
    part = jnp.sum(others.astype(F32), axis=0).astype(BF)
    return exchange(spread(part, space), "space").reshape(-1, width), *first


def on_device(
    latent,
    coords,
    cell_counts,
    pair_target,
    pair_source,
    pair_count,
    edge_target_w,
    edge_source_w,
    edge_offset,
    edge_bias,
    edge_out,
    node_in,
    node_in_bias,
    node_out,
    node_out_bias,
    norm_gain,
    cotangent,
):
    cells, particles, width = latent.shape[2:]
    core = lax.rem(lax.axis_index("wide"), 2)
    live = (
        jnp.arange(particles, dtype=jnp.int32)[None, :] < cell_counts[0, 0][:, None]
    ).astype(BF)
    meta = jnp.concatenate(
        [coords[0, 0], live[:, None, :], jnp.zeros((cells, META - 3, particles), BF)], axis=1
    )
    last = jnp.concatenate([latent[0, 0, cells - 1], meta[cells - 1]], axis=0)
    initial = jnp.concatenate([latent[0, 0, 0], meta[0]], axis=0)
    before = lax.ppermute(last, "space", neighbours("space", 1))
    after = lax.ppermute(initial, "space", neighbours("space", -1))
    scalars = (cell_counts, pair_target, pair_source, pair_count)
    state = run_own(
        scalars,
        (latent, meta, edge_target_w, edge_source_w, edge_offset, edge_bias[None, :]),
        cells,
        particles,
        width,
    )
    new_rows, partial, rims, pack = run_step(
        scalars,
        (before, after, cotangent)
        + tuple(state)
        + (
            edge_target_w,
            edge_source_w,
            edge_offset,
            edge_out,
            node_in,
            node_in_bias[None, :],
            node_out,
            node_out_bias[None, :],
            norm_gain[None, :],
        ),
        latent,
        cells,
        particles,
        width,
    )
    from_next = lax.ppermute(rims[0], "space", neighbours("space", -1))
    from_prev = lax.ppermute(rims[1], "space", neighbours("space", 1))
    mine, from_next, from_prev = sum_everywhere(pack, core, (from_next, from_prev))
    other = swap_cores(mine)
    scale = 1.0 / math.sqrt(lax.axis_size("space") * lax.axis_size("wide") * cells * particles)
    rims_in = jnp.stack([from_next, from_prev])
    outs = run_finish(
        core.astype(jnp.int32)[None], mine, other, partial, rims_in, edge_source_w, scale
    )
    (latent_grad, target_w, source_w, offset, bias, out_w, in_w, in_bias, node_w, out_bias, gain) = outs
    return (
        new_rows,
        latent_grad,
        target_w,
        source_w,
        offset,
        bias[0],
        out_w,
        in_w,
        in_bias[0],
        node_w,
        out_bias[0],
        gain[0],
    )


def solution(mesh):
    cell = P("wide", "space", None, None, None)
    table = P("wide", "space", None)
    return jax.shard_map(
        on_device,
        mesh=mesh,
        in_specs=(cell, cell, table, table, table, P("wide", "space")) + (P(),) * 10 + (cell,),
        out_specs=(cell, cell) + (P(),) * 10,
        check_vma=False,
    )
```
